128 devices in a mesh: pts: 8 (over x, core), cam: 16 (over z, y).
Axes of the slice: x: 4, y: 4, z: 4, core: 2. Of those that a mesh axis runs over, the one named last changes fastest.
Arguments:
- cam_params: float32 [9, 40960], P(None, 'cam')
- points: float32 [3, 262144], P(None, ('pts', 'cam'))
- measured: float32 [2, 8, 262144], P(None, None, ('pts', 'cam')), may hold values from -2 to 2
- obs_slot: int32 [8, 262144], P(None, ('pts', 'cam')), may hold values from 0 to 6143
- vis_tiles: int32 [128, 48], replicated, may hold values from 0 to 319, as said below
Outputs:
- camera_step: float32 [9, 40960], P(None, 'cam')
- point_step: float32 [3, 262144], P(None, ('pts', 'cam'))
The draws below stay inside these ranges and needn't reach their ends.
Inputs may be any that keep to these rules, and one draw needn't show every extreme that they name: `vis_tiles`: each row is increasing and holds exactly 3 tiles of each block of 20 consecutive tiles.
All inputs are finite; a program needn't handle non-finite values.
Results may differ from the reference program's by a relative error of at most 0.0003.
Values sent between devices are 32-bit elements; how exact they have to be, the bound alone decides.
A program may use at most 64 MiB of HBM per device.

```python
import math
import jax
import jax.numpy as jnp
from jax import lax

VIEWS = 8
ITERS = 3
PTS_DEV = 2048
TILES_DEV = 20
VIS_OWN = 3
NCAM = 40960
VIS = 48
PTS = 262144
N_PTS = 8
N_CAM = 16


def draw_cam_params(key, part):
    key = jax.random.fold_in(key, 11)
    keys = jax.random.split(key, 4)
    rotation = jax.random.uniform(keys[0], (3, NCAM), jnp.float32, -0.15, 0.15)
    offset = jax.random.uniform(keys[1], (3, NCAM), jnp.float32, -0.5, 0.5)
    focal = jnp.exp(jax.random.uniform(keys[2], (1, NCAM), jnp.float32, math.log(0.5), math.log(2.0)))
    distort = jax.random.uniform(keys[3], (2, NCAM), jnp.float32, -0.1, 0.1)
    return jnp.concatenate([rotation, offset, focal, distort], axis=0)


def draw_points(key, part):
    key = jax.random.fold_in(key, 12)
    keys = jax.random.split(key, 2)
    planar = jax.random.uniform(keys[0], (2, PTS), jnp.float32, -1.0, 1.0)
    depth = jax.random.uniform(keys[1], (1, PTS), jnp.float32, 4.0, 8.0)
    return jnp.concatenate([planar, depth], axis=0)


def draw_vis_tiles(key, part):
    key = jax.random.fold_in(key, 13)

    def one_row(index):
        subkey = jax.random.fold_in(key, index)
        scores = jax.random.randint(subkey, (N_CAM, TILES_DEV), 0, 1 << 20) * TILES_DEV + jnp.arange(TILES_DEV, dtype=jnp.int32)[None, :]
        order = jnp.argsort(scores, axis=1, stable=True)[:, :VIS_OWN]
        chosen = jnp.sort(order, axis=1) + (jnp.arange(N_CAM, dtype=jnp.int32) * TILES_DEV)[:, None]
        return chosen.reshape(-1).astype(jnp.int32)
    return jax.vmap(one_row)(jnp.arange(N_PTS * N_CAM, dtype=jnp.int32))


def plant(values, own_key, low, largest):
    shape = values.shape
    spot = [jax.random.randint(jax.random.fold_in(own_key, axis), (), 0, shape[axis]) for axis in range(len(shape))]
    values = values.at[tuple(spot)].set(low)
    longest = shape.index(max(shape))
    spot[longest] = (spot[longest] + 1) % shape[longest]
    return values.at[tuple(spot)].set(largest)


def levels(rng, shape, cuts, least, largest):
    def one(dim, parts):
        draws = jax.random.uniform(jax.random.fold_in(jax.random.fold_in(rng, 6), dim), (parts,), jnp.float32, least / len(cuts), largest / len(cuts))
        return jnp.repeat(jnp.exp(draws), shape[dim] // parts).reshape((-1,) + (1,) * (len(shape) - dim - 1))

    factor_of = one(*cuts[0])
    for cut in cuts[1:]:
        factor_of = factor_of * one(*cut)
    return factor_of


def normal_values(key, dims, width, reach, pieces=(), kind=jnp.bfloat16):
    loudness = levels(key, dims, pieces, -0.22, 0.18) if pieces else 1.0
    drawn = jax.random.normal(key, dims, jnp.float32) * width * loudness
    return jnp.minimum(jnp.maximum(drawn, -reach), reach).astype(kind)


def setup_inputs(seed: int = 0) -> dict:
    key_list = jax.random.split(jax.random.key(seed), 6)
    return {
        "cam_params": draw_cam_params(jax.random.fold_in(key_list[5], 71), 0),
        "points": draw_points(jax.random.fold_in(key_list[5], 71), 0),
        "measured": normal_values(key_list[2], (2, VIEWS, PTS), 0.3, 2.0, ((2, 128),), jnp.float32),
        "obs_slot": plant(jax.random.randint(key_list[3], (VIEWS, PTS), 0, VIS * 128), jax.random.fold_in(key_list[3], 1), 0, (VIS * 128) - 1).astype(jnp.int32),
        "vis_tiles": draw_vis_tiles(jax.random.fold_in(key_list[5], 71), 0),
    }


damping = 0.5

def project(camera, point):
    rotation = camera[0:3]
    offset = camera[3:6]
    across = jnp.cross(rotation, point)
    twice = jnp.cross(rotation, across)
    factor = 2.0 / (1.0 + jnp.sum(rotation * rotation))
    moved = point + factor * (across + twice) + offset
    plane = moved[0:2] / moved[2]
    radius = jnp.sum(plane * plane)
    return camera[6] * (1.0 + camera[7] * radius + camera[8] * radius * radius) * plane

def single_jacobian(camera, point):
    value, pull = jax.vjp(project, camera, point)
    first = pull(jnp.array([1.0, 0.0], dtype=jnp.float32))
    second = pull(jnp.array([0.0, 1.0], dtype=jnp.float32))
    return (jnp.stack([first[0], second[0]]), jnp.stack([first[1], second[1]]), value)

def linearize(cameras, pointset, observed):
    jac_cam, jac_pnt, predicted = jax.vmap(single_jacobian, in_axes=(1, 1), out_axes=-1)(cameras, pointset)
    return (jac_cam, jac_pnt, predicted - observed)

def point_inverse(jac_pnt):
    normal = lax.optimization_barrier(jnp.sum(jac_pnt[:, :, None] * jac_pnt[:, None, :], axis=(0, 3)))
    normal = normal + damping * jnp.eye(3, dtype=jnp.float32)[:, :, None]
    cofac = [[normal[1, 1] * normal[2, 2] - normal[1, 2] * normal[2, 1], normal[1, 2] * normal[2, 0] - normal[1, 0] * normal[2, 2], normal[1, 0] * normal[2, 1] - normal[1, 1] * normal[2, 0]], [normal[0, 2] * normal[2, 1] - normal[0, 1] * normal[2, 2], normal[0, 0] * normal[2, 2] - normal[0, 2] * normal[2, 0], normal[0, 1] * normal[2, 0] - normal[0, 0] * normal[2, 1]], [normal[0, 1] * normal[1, 2] - normal[0, 2] * normal[1, 1], normal[0, 2] * normal[1, 0] - normal[0, 0] * normal[1, 2], normal[0, 0] * normal[1, 1] - normal[0, 1] * normal[1, 0]]]
    determ = normal[0, 0] * cofac[0][0] + normal[0, 1] * cofac[0][1] + normal[0, 2] * cofac[0][2]
    return jnp.stack([jnp.stack([cofac[col][row] / determ for col in range(3)]) for row in range(3)])

def apply_point(inverse, vector):
    return lax.optimization_barrier(jnp.sum(inverse * vector[None, :, :], axis=1))

def cam_times(jac_cam, values):
    return lax.optimization_barrier(jnp.sum(jac_cam * values[None], axis=1))

def cam_transpose(jac_cam, values):
    return lax.optimization_barrier(jnp.sum(jac_cam * values[:, None], axis=0))

def pnt_transpose(jac_pnt, values):
    return lax.optimization_barrier(jnp.sum(jac_pnt * values[:, None], axis=(0, 2)))

def pnt_times(jac_pnt, vector):
    return lax.optimization_barrier(jnp.sum(jac_pnt * vector[None, :, None, :], axis=1))

def schur_terms(jac_cam, jac_pnt, inverse, values):
    image = cam_times(jac_cam, values)
    moved = apply_point(inverse, pnt_transpose(jac_pnt, image))
    return cam_transpose(jac_cam, image - pnt_times(jac_pnt, moved))

def right_terms(jac_cam, jac_pnt, inverse, residual):
    gradient = -pnt_transpose(jac_pnt, residual)
    moved = apply_point(inverse, gradient)
    return (cam_transpose(jac_cam, -residual - pnt_times(jac_pnt, moved)), gradient)

def reference(cam_params, points, measured, obs_slot, vis_tiles):
    views = obs_slot.shape[0]
    total = obs_slot.shape[1]
    owner = jnp.arange(total, dtype=jnp.int32) // PTS_DEV
    owner_full = jnp.broadcast_to(owner[None, :], obs_slot.shape)
    tile_ids = vis_tiles[owner_full, obs_slot // 128]
    camera_ids = (tile_ids * 128 + obs_slot % 128).reshape(-1).astype(jnp.int32)
    cams_obs = jnp.take(cam_params, camera_ids, axis=1)
    pnts_obs = jnp.broadcast_to(points[:, None, :], (3, views, total)).reshape(3, -1)
    jac_cam, jac_pnt, residual = linearize(cams_obs, pnts_obs, measured.reshape(2, -1))
    jac_cam = jac_cam.reshape(2, 9, views, total)
    jac_pnt = jac_pnt.reshape(2, 3, views, total)
    residual = residual.reshape(2, views, total)
    inverse = point_inverse(jac_pnt)

    def spread(terms):
        rows = terms.shape[0]
        return jax.ops.segment_sum(terms.reshape(rows, -1).T, camera_ids, num_segments=NCAM).T

    def on_views(vector):
        return jnp.take(vector, camera_ids, axis=1).reshape(vector.shape[0], views, total)
    right_obs, gradient = right_terms(jac_cam, jac_pnt, inverse, residual)
    rhs = spread(right_obs)
    precond = spread(lax.optimization_barrier(jnp.sum(jac_cam * jac_cam, axis=0))) + damping
    solution = jnp.zeros_like(rhs)
    remain = rhs
    scaled = remain / precond
    direction = scaled
    norm_now = jnp.sum(remain * scaled)
    for index in range(ITERS):
        image = spread(schur_terms(jac_cam, jac_pnt, inverse, on_views(direction))) + damping * direction
        alpha = norm_now / jnp.sum(direction * image)
        solution = solution + alpha * direction
        remain = remain - alpha * image
        scaled = remain / precond
        norm_next = jnp.sum(remain * scaled)
        direction = scaled + norm_next / norm_now * direction
        norm_now = norm_next
    image = cam_times(jac_cam, on_views(solution))
    point_step = apply_point(inverse, gradient - pnt_transpose(jac_pnt, image))
    return (solution, point_step)
```

```python
import functools

import jax
import jax.numpy as jnp
from jax import lax
from jax.experimental import pallas as pl
from jax.experimental.pallas import tpu as pltpu
from jax.sharding import PartitionSpec as P

MESH = pl.DeviceIdType.MESH
F32 = jnp.float32
BF16 = jnp.bfloat16
DAMPING = 0.5

NP, NC = 8, 16
ND = NP * NC
VIEWS = 8
PB = 256
NB = 8
OB = VIEWS * PB
TILES = 20
KP = 24
ROWS = 9
HI = 24
SL = ROWS * HI
PIECE = 16
SCAL = 48
PHASES = 7


def hop(step):
    return min(step, 4 - step)


OFFSETS = sorted(
    [(x, k, z, y) for x in range(4) for k in range(2) for z in range(4) for y in range(4) if x or k or z or y],
    key=lambda o: -(hop(o[0]) + hop(o[2]) + hop(o[3]) + 0.3 * o[1]),
)
PLANE = [o for o in OFFSETS if not (o[0] or o[1])]
COLUMN = [o for o in OFFSETS if not (o[2] or o[3])]


def there(offset):
    pts, cam = lax.axis_index("pts"), lax.axis_index("cam")
    dx, dk, dz, dy = offset
    x, k, z, y = pts // 2, pts % 2, cam // 4, cam % 4
    return ((x + dx) % 4) * 2 + (k + dk) % 2, ((z + dz) % 4) * 4 + (y + dy) % 4


def dot(a, b):
    return jnp.dot(a, b, preferred_element_type=F32)


def dot_nt(a, b):
    return lax.dot_general(a, b, (((1,), (1,)), ((), ())), preferred_element_type=F32)


def split(x, parts):
    out = []
    for _ in range(parts - 1):
        top = x.astype(BF16)
        out.append(top)
        x = x - top.astype(F32)
    out.append(x.astype(BF16))
    return out


def iota(shape, dim):
    return lax.broadcasted_iota(jnp.int32, shape, dim)


def total(x):
    return jnp.sum(jnp.sum(x, axis=0, keepdims=True), axis=1, keepdims=True)


def lanes(x, shift):
    shift = shift % 128
    return x if shift == 0 else pltpu.roll(x, shift, 1)


def cross(a, b):
    return (a[1] * b[2] - a[2] * b[1], a[2] * b[0] - a[0] * b[2], a[0] * b[1] - a[1] * b[0])


def dot3(a, b):
    return a[0] * b[0] + a[1] * b[1] + a[2] * b[2]


def jacobians(cam, point):
    w, t = cam[0:3], cam[3:6]
    focal, k1, k2 = cam[6:9]
    across = cross(w, point)
    twice = cross(w, across)
    turn = tuple(across[i] + twice[i] for i in range(3))
    factor = 2.0 / (1.0 + dot3(w, w))
    moved = tuple(point[i] + factor * turn[i] + t[i] for i in range(3))
    inv = 1.0 / moved[2]
    q = (moved[0] * inv, moved[1] * inv)
    s = q[0] * q[0] + q[1] * q[1]
    gain = 1.0 + k1 * s + k2 * s * s
    slope = 2.0 * focal * (k1 + 2.0 * k2 * s)
    base = focal * gain
    value = (base * q[0], base * q[1])
    mixed = slope * q[0] * q[1]
    rows = ((base + slope * q[0] * q[0], mixed), (mixed, base + slope * q[1] * q[1]))
    jac_cam, jac_pnt = [], []
    for i in range(2):
        v0, v1 = rows[i][0] * inv, rows[i][1] * inv
        v = (v0, v1, -(v0 * q[0] + v1 * q[1]))
        m = cross(v, w)
        mm = cross(m, w)
        jac_pnt.append([v[n] + factor * (m[n] + mm[n]) for n in range(3)])
        first = cross(point, tuple(v[n] + m[n] for n in range(3)))
        second = cross(across, v)
        shrink = factor * dot3(v, turn)
        rot = [factor * (first[n] + second[n] - shrink * w[n]) for n in range(3)]
        fs = focal * s * q[i]
        jac_cam.append(rot + list(v) + [gain * q[i], fs, fs * s])
    return jac_cam, jac_pnt, value


def inverse3(jac_pnt):
    n = [[None] * 3 for _ in range(3)]
    for a in range(3):
        for b in range(a, 3):
            whole = jnp.sum(jac_pnt[0][a] * jac_pnt[0][b] + jac_pnt[1][a] * jac_pnt[1][b], axis=0, keepdims=True)
            n[a][b] = n[b][a] = whole + DAMPING if a == b else whole
    c00 = n[1][1] * n[2][2] - n[1][2] * n[2][1]
    c01 = n[1][2] * n[2][0] - n[1][0] * n[2][2]
    c02 = n[1][0] * n[2][1] - n[1][1] * n[2][0]
    c11 = n[0][0] * n[2][2] - n[0][2] * n[2][0]
    c12 = n[0][1] * n[2][0] - n[0][0] * n[2][1]
    c22 = n[0][0] * n[1][1] - n[0][1] * n[1][0]
    r = 1.0 / (n[0][0] * c00 + n[0][1] * c01 + n[0][2] * c02)
    return [c00 * r, c01 * r, c02 * r, c11 * r, c12 * r, c22 * r]


def apply_inverse(inv, v):
    return (
        inv[0] * v[0] + inv[1] * v[1] + inv[2] * v[2],
        inv[1] * v[0] + inv[3] * v[1] + inv[4] * v[2],
        inv[2] * v[0] + inv[4] * v[1] + inv[5] * v[2],
    )


def kernel(
    vis_s, vis_v, cam_ref, pts_ref, meas_ref, slot_ref,
    cam_out, pnt_out,
    camt, src0, dst0, src, dst, fsrc, fdst, srcx, dstx,
    hot, hid_ref, y_ref, t_ref, jc_ref, jp_ref, inv_ref, grad_ref, w_ref, terms_ref,
    gath, cols, acc, acc2, z_ref, d_ref, vt_ref, sel, selt, s1o, d2o, uq,
    sem0, sends, recvs, fsem, semx, ready,
):
    pts, cam = lax.axis_index("pts"), lax.axis_index("cam")
    me = pts * NC + cam

    barrier = pltpu.get_barrier_semaphore()
    for offset in PLANE + COLUMN:
        pl.semaphore_signal(barrier, inc=1, device_id=there(offset), device_id_type=MESH)

    for k in range(TILES):
        camt[k, 0:9, :] = cam_ref[:, k * 128 : (k + 1) * 128]
    for c in range(NC):
        for j in range(3):
            one = camt[jnp.clip(vis_s[pts * NC + c, 3 * cam + j] - TILES * cam, 0, TILES - 1)]
            src0[c, j] = one[0:8]
            src0[c, 3, j : j + 1, :] = one[8:9]

    def build(b, _):
        slot = slot_ref[:, pl.ds(pl.multiple_of(b * PB, PB), PB)]
        place = slot // 128
        shard = (place * 171) // 512
        own = place - 3 * shard
        half = shard // 8
        hid_ref[b] = own * 8 + shard - 8 * half
        low = half * 128 + slot - 128 * place
        for v in range(VIEWS):
            row = jnp.broadcast_to(low[v : v + 1, :], (256, PB))
            hot[b, :, v * PB : (v + 1) * PB] = (row == iota((256, PB), 0)).astype(F32).astype(BF16)
        return 0

    lax.fori_loop(0, NB, build, 0)

    vt_ref[...] = jnp.zeros((128, 128), F32)
    vt_ref[:, 0:48] = vis_v[...].astype(F32)
    vt_ref[...] = vt_ref[...].T
    spread_rows = []
    for t in range(3):
        row = vt_ref[pl.ds(3 * cam + t, 1), :] - (TILES * cam).astype(F32)
        row = jnp.broadcast_to(row, (8, 128)).astype(BF16)
        put = ((iota((128, 512), 1) // 4) == iota((128, 512), 0)).astype(F32).astype(BF16)
        spread_rows.append(dot(row, put)[0:1, :])
    quarter = iota((1, 512), 1) % 4
    index = jnp.where(quarter == 0, spread_rows[0], jnp.where(quarter == 1, spread_rows[1], spread_rows[2]))
    index = jnp.where(quarter == 3, -1.0, index)
    tile_no = iota((KP, 512), 0).astype(F32)
    blocks = [(jnp.broadcast_to(index, (KP, 512)) == tile_no).astype(F32)]
    for t in range(3):
        this = jnp.where(quarter == 3, spread_rows[t], -1.0)
        blocks.append((jnp.broadcast_to(this, (KP, 512)) == tile_no).astype(F32))
    blocks.append(jnp.zeros((128 - 4 * KP, 512), F32))
    pick = jnp.concatenate(blocks, axis=0)
    sel[...] = pick.astype(BF16)
    selt[...] = pick.T.astype(BF16)

    pl.semaphore_wait(barrier, len(PLANE) + len(COLUMN))
    for offset in COLUMN:
        pl.semaphore_signal(ready, inc=1, device_id=there(offset), device_id_type=MESH)
    for offset in PLANE:
        _, c = there(offset)
        pltpu.make_async_remote_copy(
            src0.at[c], dst0.at[cam], sem0.at[0], sem0.at[1], device_id=(pts, c), device_id_type=MESH
        ).start()
    dst0[cam] = src0[cam]
    pltpu.make_async_copy(src0.at[pl.ds(0, 15)], dst0.at[pl.ds(0, 15)], sem0.at[1]).wait()
    pl.semaphore_wait(ready, len(COLUMN))

    def send(phase):
        for offset in OFFSETS:
            p, c = there(offset)
            to = p * NC + c
            pltpu.make_async_remote_copy(
                src.at[phase, to], dst.at[phase, me], sends.at[phase], recvs.at[phase],
                device_id=(p, c), device_id_type=MESH,
            ).start()
        dst[phase, me] = src[phase, me]

    def arrived(phase):
        pltpu.make_async_copy(
            src.at[phase, pl.ds(0, ND - 1)], dst.at[phase, pl.ds(0, ND - 1)], recvs.at[phase]
        ).wait()

    def sent(phase):
        pltpu.make_async_copy(
            src.at[phase, pl.ds(0, ND - 1)], dst.at[phase, pl.ds(0, ND - 1)], sends.at[phase]
        ).wait()

    lane = iota((1, 128), 1)

    def send_collect(phase, from_ref):
        for r in range(8):
            for j in range(3):
                for half in range(2):
                    src[phase, r * 16 + half * 8 : r * 16 + half * 8 + 8, j, :] = from_ref[
                        r * HI + j * 8 : r * HI + j * 8 + 8, half * 128 : half * 128 + 128
                    ]
        for half in range(2):
            last = [
                from_ref[8 * HI + j * 8 : 8 * HI + j * 8 + 8, half * 128 : half * 128 + 128] for j in range(3)
            ]
            for p in range(NP):
                row = jnp.zeros((8, 128), F32)
                for j in range(3):
                    row = jnp.where(lane // PIECE == j, lanes(last[j], PIECE * (j - p)), row)
                src[phase, p * 16 + half * 8 : p * 16 + half * 8 + 8, 3, :] = row
        send(phase)

    def recv_collect(phase):
        arrived(phase)
        flat = dst[phase].reshape(ND * 4, 128)
        got = sum(dot(sel[...], part) for part in split(flat, 3))
        row8 = sum(lanes(got[KP * (t + 1) : KP * (t + 2)], -PIECE * t) for t in range(3))
        row8 = jnp.where(lane < PIECE, row8, 0.0)
        return jnp.concatenate([got[0:KP], row8], axis=0)

    def send_deliver(phase, own, dots):
        rows = [own[0:KP]] + [lanes(own[KP:], PIECE * t) for t in range(3)]
        rows.append(jnp.zeros((128 - 4 * KP, 128), F32))
        stacked = jnp.concatenate(rows, axis=0)
        out = sum(dot(selt[...], part) for part in split(stacked, 3))
        note = jnp.zeros((1, 128), F32)
        for i, value in enumerate(dots):
            note = jnp.where(lane == SCAL + i, value, note)
        out = out + jnp.where(iota((512, 128), 0) % 4 == 3, note, 0.0)
        src[phase] = out.reshape(ND, 4, 128)
        send(phase)

    def recv_deliver(phase, to_ref):
        arrived(phase)
        notes = jnp.zeros((8, 128), F32)
        for half in range(2):
            for r in range(8):
                for j in range(3):
                    to_ref[r * HI + j * 8 : r * HI + j * 8 + 8, half * 128 : half * 128 + 128] = dst[
                        phase, r * 16 + half * 8 : r * 16 + half * 8 + 8, j, :
                    ]
            last = [jnp.zeros((8, 128), F32)] * 3
            for p in range(NP):
                row = dst[phase, p * 16 + half * 8 : p * 16 + half * 8 + 8, 3, :]
                notes = notes + row
                for j in range(3):
                    last[j] = jnp.where(lane // PIECE == p, lanes(row, PIECE * (p - j)), last[j])
            for j in range(3):
                to_ref[8 * HI + j * 8 : 8 * HI + j * 8 + 8, half * 128 : half * 128 + 128] = last[j]
        notes = jnp.sum(notes, axis=0, keepdims=True)
        return [jnp.sum(jnp.where(lane == SCAL + i, notes, 0.0), axis=1, keepdims=True) for i in range(4)]

    def load_columns(x, parts):
        for i, part in enumerate(split(x, parts)):
            cols[i] = part

    def gather(b, parts):
        y_ref[...] = sum(dot(cols[i], hot[b]) for i in range(parts))
        hid = hid_ref[b]
        for v in range(VIEWS):
            mask = jnp.broadcast_to(hid[v : v + 1, :], (HI, PB)) == iota((HI, PB), 0)
            for r in range(ROWS):
                piece = y_ref[r * HI : (r + 1) * HI, v * PB : (v + 1) * PB]
                gath[r, v : v + 1, :] = jnp.sum(jnp.where(mask, piece, 0.0), axis=0, keepdims=True)
        return [gath[r] for r in range(ROWS)]

    def scatter(b, terms, to_ref):
        hid = hid_ref[b]
        for r in range(ROWS):
            top = terms[r].astype(BF16).astype(F32)
            terms_ref[r] = top
            terms_ref[ROWS + r] = terms[r] - top
        for v in range(VIEWS):
            mask = jnp.broadcast_to(hid[v : v + 1, :], (HI, PB)) == iota((HI, PB), 0)
            for r in range(2 * ROWS):
                row = jnp.broadcast_to(terms_ref[r, v : v + 1, :], (HI, PB))
                t_ref[r * HI : (r + 1) * HI, v * PB : (v + 1) * PB] = jnp.where(mask, row, 0.0).astype(BF16)
        both = dot_nt(t_ref[...], hot[b])
        to_ref[...] += both[0:SL] + both[SL:]

    for half in range(2):
        for j in range(3):
            for r in range(8):
                d_ref[r * HI + j * 8 : r * HI + j * 8 + 8, half * 128 : half * 128 + 128] = dst0[
                    half * 8 : half * 8 + 8, j, r, :
                ]
            d_ref[8 * HI + j * 8 : 8 * HI + j * 8 + 8, half * 128 : half * 128 + 128] = dst0[
                half * 8 : half * 8 + 8, 3, j, :
            ]
    load_columns(d_ref[...], 3)
    acc[...] = jnp.zeros_like(acc)
    acc2[...] = jnp.zeros_like(acc2)

    def linearize(b, _):
        at = pl.ds(pl.multiple_of(b * PB, PB), PB)
        cams = gather(b, 3)
        point = tuple(jnp.broadcast_to(pts_ref[i : i + 1, at], (VIEWS, PB)) for i in range(3))
        jac_cam, jac_pnt, value = jacobians(cams, point)
        residual = [value[i] - meas_ref[i, :, at] for i in range(2)]
        inv = inverse3(jac_pnt)
        grad = [
            -jnp.sum(jac_pnt[0][n] * residual[0] + jac_pnt[1][n] * residual[1], axis=0, keepdims=True)
            for n in range(3)
        ]
        moved = apply_inverse(inv, grad)
        for i in range(2):
            for r in range(ROWS):
                jc_ref[b, i * ROWS + r] = jac_cam[i][r]
            for n in range(3):
                jp_ref[b, i * 3 + n] = jac_pnt[i][n]
        for n in range(6):
            inv_ref[b, n : n + 1, :] = inv[n]
        for n in range(3):
            grad_ref[b, n : n + 1, :] = grad[n]
        left = [-residual[i] - dot3(jac_pnt[i], moved) for i in range(2)]
        scatter(b, [jac_cam[0][r] * jac_cam[0][r] + jac_cam[1][r] * jac_cam[1][r] for r in range(ROWS)], acc2)
        scatter(b, [jac_cam[0][r] * left[0] + jac_cam[1][r] * left[1] for r in range(ROWS)], acc)
        return 0

    lax.fori_loop(0, NB, linearize, 0)
    send_collect(0, acc2)
    send_collect(1, acc)
    precond = recv_collect(0) + DAMPING
    remain = recv_collect(1)
    scaled = remain / precond
    direction = scaled
    send_deliver(2, scaled, [total(remain * scaled)])

    norm = recv_deliver(2, z_ref)[0]
    d_ref[...] = z_ref[...]

    def apply(b, step, last):
        dirs = gather(b, 2)
        jac = [[jc_ref[b, i * ROWS + r] for r in range(ROWS)] for i in range(2)]
        jac_pnt = [[jp_ref[b, i * 3 + n] for n in range(3)] for i in range(2)]
        u = []
        for i in range(2):
            value = jac[i][0] * dirs[0]
            for r in range(1, ROWS):
                value = value + jac[i][r] * dirs[r]
            u.append(value)
        w = [jnp.sum(jac_pnt[0][n] * u[0] + jac_pnt[1][n] * u[1], axis=0, keepdims=True) for n in range(3)]
        for n in range(3):
            w_ref[step, b, n : n + 1, :] = w[n]
        moved = apply_inverse([inv_ref[b, n : n + 1, :] for n in range(6)], w)
        left = [u[i] - dot3(jac_pnt[i], moved) for i in range(2)]
        if last:
            uq[...] += u[0] * left[0] + u[1] * left[1]
        else:
            scatter(b, [jac[0][r] * left[0] + jac[1][r] * left[1] for r in range(ROWS)], acc)
        return 0

    solved = None
    alphas = []
    for step in range(2):
        load_columns(d_ref[...], 2)
        acc[...] = jnp.zeros_like(acc)
        lax.fori_loop(0, NB, lambda b, _: apply(b, step, False), 0)
        send_collect(3 + 2 * step, acc)
        image = recv_collect(3 + 2 * step) + DAMPING * direction
        quot = image / precond
        send_deliver(
            4 + 2 * step, quot,
            [total(remain * scaled), total(direction * image), total(scaled * image), total(quot * image)],
        )
        rz, dim, zim, imq = recv_deliver(4 + 2 * step, acc2)
        alpha = rz / dim
        beta = (rz - 2.0 * alpha * zim + alpha * alpha * imq) / rz
        z_ref[...] = z_ref[...] - alpha * acc2[...]
        d_ref[...] = z_ref[...] + beta * d_ref[...]
        solved = alpha * direction if step == 0 else solved + alpha * direction
        remain = remain - alpha * image
        scaled = remain / precond
        direction = scaled + beta * direction
        alphas.append(alpha)

    srcx[0, 0:KP] = solved[0:KP]
    srcx[0, KP : 2 * KP] = direction[0:KP]
    srcx[0, 2 * KP :] = solved[KP:] + lanes(direction[KP:], PIECE)
    for offset in COLUMN:
        p, _ = there(offset)
        pltpu.make_async_remote_copy(
            srcx.at[0], dstx.at[pts], semx.at[0], semx.at[1], device_id=(p, cam), device_id_type=MESH
        ).start()
    dstx[pts] = srcx[0]
    load_columns(d_ref[...], 2)
    uq[...] = jnp.zeros_like(uq)
    lax.fori_loop(0, NB, lambda b, _: apply(b, 2, True), 0)
    mine = total(uq[...]) + DAMPING * total(direction * direction)
    norm = total(remain * scaled)
    fsrc[...] = jnp.where(lane == 0, mine, jnp.where(lane == 1, norm, 0.0)).reshape(1, 1, 128)
    for offset in OFFSETS:
        p, c = there(offset)
        pltpu.make_async_remote_copy(
            fsrc.at[0], fdst.at[me], fsem.at[0], fsem.at[1], device_id=(p, c), device_id_type=MESH
        ).start()
    fdst[me] = fsrc[0]

    pltpu.make_async_copy(dstx.at[pl.ds(0, 7)], dstx.at[pl.ds(0, 7)], semx.at[1]).wait()
    for part, out in ((0, s1o), (1, d2o)):
        tail = jnp.zeros((KP, 128), F32)
        for p in range(NP):
            tail = jnp.where(lane // PIECE == p, lanes(dstx[p, 2 * KP :], PIECE * (p - part)), tail)
        for k in range(TILES):
            out[0:8, k * 128 : (k + 1) * 128] = dstx[:, part * KP + k, :]
            out[8:9, k * 128 : (k + 1) * 128] = tail[k : k + 1]

    pltpu.make_async_copy(fdst.at[pl.ds(0, ND - 1)], fdst.at[pl.ds(0, ND - 1)], fsem.at[1]).wait()
    sums = jnp.sum(fdst[...], axis=0)
    dim = jnp.sum(jnp.where(lane == 0, sums, 0.0), axis=1, keepdims=True)
    rz = jnp.sum(jnp.where(lane == 1, sums, 0.0), axis=1, keepdims=True)
    alpha = rz / dim
    alphas.append(alpha)
    cam_out[...] = s1o[...] + alpha * d2o[...]
    for b in range(NB):
        left = []
        for n in range(3):
            value = grad_ref[b, n : n + 1, :]
            for step in range(3):
                value = value - alphas[step] * w_ref[step, b, n : n + 1, :]
            left.append(value)
        out = apply_inverse([inv_ref[b, n : n + 1, :] for n in range(6)], left)
        for n in range(3):
            pnt_out[n : n + 1, b * PB : (b + 1) * PB] = out[n]

    pltpu.make_async_copy(src0.at[pl.ds(0, 15)], dst0.at[pl.ds(0, 15)], sem0.at[0]).wait()
    for phase in range(PHASES):
        sent(phase)
    pltpu.make_async_copy(dstx.at[pl.ds(0, 7)], dstx.at[pl.ds(0, 7)], semx.at[0]).wait()
    pltpu.make_async_copy(fdst.at[pl.ds(0, ND - 1)], fdst.at[pl.ds(0, ND - 1)], fsem.at[0]).wait()


def shards(cam_params, points, measured, obs_slot, vis_tiles):
    vmem = pl.BlockSpec(memory_space=pltpu.VMEM)
    dma = pltpu.SemaphoreType.DMA
    return pl.pallas_call(
        kernel,
        out_shape=(
            jax.ShapeDtypeStruct(cam_params.shape, F32),
            jax.ShapeDtypeStruct(points.shape, F32),
        ),
        in_specs=[pl.BlockSpec(memory_space=pltpu.SMEM)] + [vmem] * 5,
        out_specs=(vmem, vmem),
        scratch_shapes=[
            pltpu.VMEM((TILES, 16, 128), F32),
            pltpu.VMEM((NC, 4, 8, 128), F32),
            pltpu.VMEM((NC, 4, 8, 128), F32),
            pltpu.VMEM((PHASES, ND, 4, 128), F32),
            pltpu.VMEM((PHASES, ND, 4, 128), F32),
            pltpu.VMEM((1, 1, 128), F32),
            pltpu.VMEM((ND, 1, 128), F32),
            pltpu.VMEM((1, 3 * KP, 128), F32),
            pltpu.VMEM((NP, 3 * KP, 128), F32),
            pltpu.VMEM((NB, 256, OB), BF16),
            pltpu.VMEM((NB, VIEWS, PB), jnp.int32),
            pltpu.VMEM((SL, OB), F32),
            pltpu.VMEM((2 * SL, OB), BF16),
            pltpu.VMEM((NB, 2 * ROWS, VIEWS, PB), F32),
            pltpu.VMEM((NB, 6, VIEWS, PB), F32),
            pltpu.VMEM((NB, 8, PB), F32),
            pltpu.VMEM((NB, 8, PB), F32),
            pltpu.VMEM((3, NB, 8, PB), F32),
            pltpu.VMEM((2 * ROWS, VIEWS, PB), F32),
            pltpu.VMEM((ROWS, VIEWS, PB), F32),
            pltpu.VMEM((3, SL, 256), BF16),
            pltpu.VMEM((SL, 256), F32),
            pltpu.VMEM((SL, 256), F32),
            pltpu.VMEM((SL, 256), F32),
            pltpu.VMEM((SL, 256), F32),
            pltpu.VMEM((128, 128), F32),
            pltpu.VMEM((128, 512), BF16),
            pltpu.VMEM((512, 128), BF16),
            pltpu.VMEM((ROWS, TILES * 128), F32),
            pltpu.VMEM((ROWS, TILES * 128), F32),
            pltpu.VMEM((VIEWS, PB), F32),
            dma((2,)),
            dma((PHASES,)),
            dma((PHASES,)),
            dma((2,)),
            dma((2,)),
            pltpu.SemaphoreType.REGULAR,
        ],
        compiler_params=pltpu.CompilerParams(
            collective_id=0, has_side_effects=True, vmem_limit_bytes=60 << 20
        ),
    )(vis_tiles, vis_tiles, cam_params, points, measured, obs_slot)


def solution(mesh):
    placed = (
        P(None, "cam"),
        P(None, ("pts", "cam")),
        P(None, None, ("pts", "cam")),
        P(None, ("pts", "cam")),
        P(),
    )
    return jax.shard_map(
        shards,
        mesh=mesh,
        in_specs=placed,
        out_specs=(P(None, "cam"), P(None, ("pts", "cam"))),
        check_vma=False,
    )
```

```python
import functools

import jax
import jax.numpy as jnp
from jax import lax
from jax.experimental import pallas as pl
from jax.experimental.pallas import tpu as pltpu
from jax.sharding import PartitionSpec as P

MESH = pl.DeviceIdType.MESH
F32 = jnp.float32
BF16 = jnp.bfloat16
DAMPING = 0.5

NP, NC = 8, 16
ND = NP * NC
VIEWS = 8
PB = 256
NB = 8
OB = VIEWS * PB
TILES = 20
KP = 24
ROWS = 9
HI = 24
SL = ROWS * HI
PIECE = 16
SCAL = 48
PHASES = 7


def hop(step):
    return min(step, 4 - step)


OFFSETS = sorted(
    [(x, k, z, y) for x in range(4) for k in range(2) for z in range(4) for y in range(4) if x or k or z or y],
    key=lambda o: -(hop(o[0]) + hop(o[2]) + hop(o[3]) + 0.3 * o[1]),
)
PLANE = [o for o in OFFSETS if not (o[0] or o[1])]
COLUMN = [o for o in OFFSETS if not (o[2] or o[3])]


def neighbours():
    pts, cam = lax.axis_index("pts"), lax.axis_index("cam")
    x, k = lax.div(pts, 2), lax.rem(pts, 2)
    z, y = lax.div(cam, 4), lax.rem(cam, 4)
    xs = [lax.rem(x + d, 4) * 2 for d in range(4)]
    ks = [k, 1 - k]
    zs = [lax.rem(z + d, 4) * 4 for d in range(4)]
    ys = [lax.rem(y + d, 4) for d in range(4)]
    columns = {(dx, dk): xs[dx] + ks[dk] for dx in range(4) for dk in range(2)}
    planes = {(dz, dy): zs[dz] + ys[dy] for dz in range(4) for dy in range(4)}
    return lambda o: (columns[o[0], o[1]], planes[o[2], o[3]])


def message(ref, index, rows):
    return ref.at[pl.ds(pl.multiple_of(index * rows, rows), rows), :]


def dot(a, b):
    return jnp.dot(a, b, preferred_element_type=F32)


def dot_nt(a, b):
    return lax.dot_general(a, b, (((1,), (1,)), ((), ())), preferred_element_type=F32)


def split(x, parts):
    out = []
    for _ in range(parts - 1):
        top = x.astype(BF16)
        out.append(top)
        x = x - top.astype(F32)
    out.append(x.astype(BF16))
    return out


def iota(shape, dim):
    return lax.broadcasted_iota(jnp.int32, shape, dim)


def total(x):
    return jnp.sum(jnp.sum(x, axis=0, keepdims=True), axis=1, keepdims=True)


def lanes(x, shift):
    shift = shift % 128
    return x if shift == 0 else pltpu.roll(x, shift, 1)


def cross(a, b):
    return (a[1] * b[2] - a[2] * b[1], a[2] * b[0] - a[0] * b[2], a[0] * b[1] - a[1] * b[0])


def dot3(a, b):
    return a[0] * b[0] + a[1] * b[1] + a[2] * b[2]


def jacobians(cam, point):
    w, t = cam[0:3], cam[3:6]
    focal, k1, k2 = cam[6:9]
    across = cross(w, point)
    twice = cross(w, across)
    turn = tuple(across[i] + twice[i] for i in range(3))
    factor = 2.0 / (1.0 + dot3(w, w))
    moved = tuple(point[i] + factor * turn[i] + t[i] for i in range(3))
    inv = 1.0 / moved[2]
    q = (moved[0] * inv, moved[1] * inv)
    s = q[0] * q[0] + q[1] * q[1]
    gain = 1.0 + k1 * s + k2 * s * s
    slope = 2.0 * focal * (k1 + 2.0 * k2 * s)
    base = focal * gain
    value = (base * q[0], base * q[1])
    mixed = slope * q[0] * q[1]
    rows = ((base + slope * q[0] * q[0], mixed), (mixed, base + slope * q[1] * q[1]))
    jac_cam, jac_pnt = [], []
    for i in range(2):
        v0, v1 = rows[i][0] * inv, rows[i][1] * inv
        v = (v0, v1, -(v0 * q[0] + v1 * q[1]))
        m = cross(v, w)
        mm = cross(m, w)
        jac_pnt.append([v[n] + factor * (m[n] + mm[n]) for n in range(3)])
        first = cross(point, tuple(v[n] + m[n] for n in range(3)))
        second = cross(across, v)
        shrink = factor * dot3(v, turn)
        rot = [factor * (first[n] + second[n] - shrink * w[n]) for n in range(3)]
        fs = focal * s * q[i]
        jac_cam.append(rot + list(v) + [gain * q[i], fs, fs * s])
    return jac_cam, jac_pnt, value


def inverse3(jac_pnt):
    n = [[None] * 3 for _ in range(3)]
    for a in range(3):
        for b in range(a, 3):
            whole = jnp.sum(jac_pnt[0][a] * jac_pnt[0][b] + jac_pnt[1][a] * jac_pnt[1][b], axis=0, keepdims=True)
            n[a][b] = n[b][a] = whole + DAMPING if a == b else whole
    c00 = n[1][1] * n[2][2] - n[1][2] * n[2][1]
    c01 = n[1][2] * n[2][0] - n[1][0] * n[2][2]
    c02 = n[1][0] * n[2][1] - n[1][1] * n[2][0]
    c11 = n[0][0] * n[2][2] - n[0][2] * n[2][0]
    c12 = n[0][1] * n[2][0] - n[0][0] * n[2][1]
    c22 = n[0][0] * n[1][1] - n[0][1] * n[1][0]
    r = 1.0 / (n[0][0] * c00 + n[0][1] * c01 + n[0][2] * c02)
    return [c00 * r, c01 * r, c02 * r, c11 * r, c12 * r, c22 * r]


def apply_inverse(inv, v):
    return (
        inv[0] * v[0] + inv[1] * v[1] + inv[2] * v[2],
        inv[1] * v[0] + inv[3] * v[1] + inv[4] * v[2],
        inv[2] * v[0] + inv[4] * v[1] + inv[5] * v[2],
    )


def kernel(
    vis_s, vis_v, cam_ref, pts_ref, meas_ref, slot_ref,
    cam_out, pnt_out,
    camt, src0, dst0, src, dst, fsrc, fdst, srcx, dstx,
    hot, hid_ref, t_ref, jc_ref, jp_ref, inv_ref, grad_ref, w_ref, terms_ref,
    gath, cols, acc, acc2, z_ref, d_ref, sel, selt, s1o, d2o, p0_ref, p2_ref, uq,
    sem0, sends, recvs, fsem, semx, ready,
):
    pts, cam = lax.axis_index("pts"), lax.axis_index("cam")
    me = pts * NC + cam
    there = neighbours()

    barrier = pltpu.get_barrier_semaphore()
    for offset in PLANE + COLUMN:
        pl.semaphore_signal(barrier, inc=1, device_id=there(offset), device_id_type=MESH)

    for k in range(TILES):
        camt[k, 0:9, :] = cam_ref[:, k * 128 : (k + 1) * 128]
    for c in range(NC):
        for j in range(3):
            one = camt[jnp.clip(vis_s[3 * cam + j, pts * NC + c] - TILES * cam, 0, TILES - 1)]
            src0[c * 32 + j * 8 : c * 32 + j * 8 + 8, :] = one[0:8]
            src0[c * 32 + 24 + j : c * 32 + 25 + j, :] = one[8:9]

    def build(b, _):
        slot = slot_ref[:, pl.ds(pl.multiple_of(b * PB, PB), PB)]
        place = slot // 128
        shard = (place * 171) // 512
        own = place - 3 * shard
        half = shard // 8
        hid_ref[b] = own * 8 + shard - 8 * half
        low = half * 128 + slot - 128 * place
        for v in range(VIEWS):
            row = jnp.broadcast_to(low[v : v + 1, :], (256, PB))
            hot[b, :, v * PB : (v + 1) * PB] = (row == iota((256, PB), 0)).astype(F32).astype(BF16)
        return 0

    lax.fori_loop(0, NB, build, 0)

    spread_rows = []
    for t in range(3):
        row = (vis_v[pl.ds(3 * cam + t, 1), :] - TILES * cam).astype(F32)
        row = jnp.broadcast_to(row, (8, 128)).astype(BF16)
        put = ((iota((128, 512), 1) // 4) == iota((128, 512), 0)).astype(F32).astype(BF16)
        spread_rows.append(dot(row, put)[0:1, :])
    quarter = iota((1, 512), 1) % 4
    index = jnp.where(quarter == 0, spread_rows[0], jnp.where(quarter == 1, spread_rows[1], spread_rows[2]))
    index = jnp.where(quarter == 3, -1.0, index)
    tile_no = iota((KP, 512), 0).astype(F32)
    blocks = [(jnp.broadcast_to(index, (KP, 512)) == tile_no).astype(F32)]
    for t in range(3):
        this = jnp.where(quarter == 3, spread_rows[t], -1.0)
        blocks.append((jnp.broadcast_to(this, (KP, 512)) == tile_no).astype(F32))
    blocks.append(jnp.zeros((128 - 4 * KP, 512), F32))
    pick = jnp.concatenate(blocks, axis=0)
    sel[...] = pick.astype(BF16)
    selt[...] = pick.T.astype(BF16)

    pl.semaphore_wait(barrier, len(PLANE) + len(COLUMN))
    for offset in COLUMN:
        pl.semaphore_signal(ready, inc=1, device_id=there(offset), device_id_type=MESH)
    for offset in PLANE:
        _, c = there(offset)
        pltpu.make_async_remote_copy(
            message(src0, c, 32), message(dst0, cam, 32), sem0.at[0], sem0.at[1],
            device_id=(pts, c), device_id_type=MESH,
        ).start()
    pltpu.make_async_copy(message(src0, cam, 32), message(dst0, cam, 32), sem0.at[1]).start()
    pltpu.make_async_copy(src0, dst0, sem0.at[1]).wait()
    pl.semaphore_wait(ready, len(COLUMN))

    def send(phase):
        for offset in OFFSETS:
            p, c = there(offset)
            to = p * NC + c
            pltpu.make_async_remote_copy(
                message(src.at[phase], to, 4), message(dst.at[phase], me, 4), sends.at[phase], recvs.at[phase],
                device_id=(p, c), device_id_type=MESH,
            ).start()
        pltpu.make_async_copy(message(src.at[phase], me, 4), message(dst.at[phase], me, 4), recvs.at[phase]).start()

    def arrived(phase):
        pltpu.make_async_copy(src.at[phase], dst.at[phase], recvs.at[phase]).wait()

    def sent(phase):
        rows = pl.ds(0, 4 * ND - 4)
        pltpu.make_async_copy(src.at[phase, rows], dst.at[phase, rows], sends.at[phase]).wait()

    lane = iota((1, 128), 1)

    def send_collect(phase, from_ref):
        for r in range(8):
            for j in range(3):
                for half in range(2):
                    src[phase, pl.ds(r * 64 + half * 32 + j, 8, stride=4), :] = from_ref[
                        r * HI + j * 8 : r * HI + j * 8 + 8, half * 128 : half * 128 + 128
                    ]
        for half in range(2):
            last = [
                from_ref[8 * HI + j * 8 : 8 * HI + j * 8 + 8, half * 128 : half * 128 + 128] for j in range(3)
            ]
            for p in range(NP):
                row = jnp.zeros((8, 128), F32)
                for j in range(3):
                    row = jnp.where(lane // PIECE == j, lanes(last[j], PIECE * (j - p)), row)
                src[phase, pl.ds(p * 64 + half * 32 + 3, 8, stride=4), :] = row
        send(phase)

    def recv_collect(phase):
        arrived(phase)
        got = sum(dot(sel[...], part) for part in split(dst[phase], 3))
        row8 = sum(lanes(got[KP * (t + 1) : KP * (t + 2)], -PIECE * t) for t in range(3))
        row8 = jnp.where(lane < PIECE, row8, 0.0)
        return jnp.concatenate([got[0:KP], row8], axis=0)

    def send_deliver(phase, own, dots):
        rows = [own[0:KP]] + [lanes(own[KP:], PIECE * t) for t in range(3)]
        rows.append(jnp.zeros((128 - 4 * KP, 128), F32))
        stacked = jnp.concatenate(rows, axis=0)
        out = sum(dot(selt[...], part) for part in split(stacked, 3))
        note = jnp.zeros((1, 128), F32)
        for i, value in enumerate(dots):
            note = jnp.where(lane == SCAL + i, value, note)
        out = out + jnp.where(iota((512, 128), 0) % 4 == 3, note, 0.0)
        src[phase] = out
        send(phase)

    def recv_deliver(phase, to_ref):
        arrived(phase)
        notes = jnp.zeros((8, 128), F32)
        for half in range(2):
            for r in range(8):
                for j in range(3):
                    to_ref[r * HI + j * 8 : r * HI + j * 8 + 8, half * 128 : half * 128 + 128] = dst[
                        phase, pl.ds(r * 64 + half * 32 + j, 8, stride=4), :
                    ]
            last = [jnp.zeros((8, 128), F32)] * 3
            for p in range(NP):
                row = dst[phase, pl.ds(p * 64 + half * 32 + 3, 8, stride=4), :]
                notes = notes + row
                for j in range(3):
                    last[j] = jnp.where(lane // PIECE == p, lanes(row, PIECE * (p - j)), last[j])
            for j in range(3):
                to_ref[8 * HI + j * 8 : 8 * HI + j * 8 + 8, half * 128 : half * 128 + 128] = last[j]
        notes = jnp.sum(notes, axis=0, keepdims=True)
        return [jnp.sum(jnp.where(lane == SCAL + i, notes, 0.0), axis=1, keepdims=True) for i in range(4)]

    def load_columns(x, parts):
        for i, part in enumerate(split(x, parts)):
            cols[i] = part

    def gather(b, k, parts):
        hid = hid_ref[b]
        for v in range(VIEWS):
            column = hot[b, :, v * PB : (v + 1) * PB]
            found = sum(dot(cols[i], column) for i in range(parts))
            mask = jnp.broadcast_to(hid[v : v + 1, :], (HI, PB)) == iota((HI, PB), 0)
            for r in range(ROWS):
                piece = found[r * HI : (r + 1) * HI]
                gath[k, r, v : v + 1, :] = jnp.sum(jnp.where(mask, piece, 0.0), axis=0, keepdims=True)

    def scatter(b, k, terms, to_ref):
        hid = hid_ref[b]
        count = len(terms)
        for r in range(count):
            top = terms[r].astype(BF16).astype(F32)
            terms_ref[k, r] = top
            terms_ref[k, count + r] = terms[r] - top
        for v in range(VIEWS):
            mask = jnp.broadcast_to(hid[v : v + 1, :], (HI, PB)) == iota((HI, PB), 0)
            for r in range(2 * count):
                row = jnp.broadcast_to(terms_ref[k, r, v : v + 1, :], (HI, PB))
                t_ref[k, r * HI : (r + 1) * HI, v * PB : (v + 1) * PB] = jnp.where(mask, row, 0.0).astype(BF16)
        both = dot_nt(t_ref[k, 0 : 2 * count * HI], hot[b])
        to_ref[0 : count * HI] += both[0 : count * HI] + both[count * HI :]

    for half in range(2):
        for j in range(3):
            for r in range(8):
                d_ref[r * HI + j * 8 : r * HI + j * 8 + 8, half * 128 : half * 128 + 128] = dst0[
                    pl.ds(half * 256 + j * 8 + r, 8, stride=32), :
                ]
            d_ref[8 * HI + j * 8 : 8 * HI + j * 8 + 8, half * 128 : half * 128 + 128] = dst0[
                pl.ds(half * 256 + 24 + j, 8, stride=32), :
            ]
    load_columns(d_ref[...], 3)
    acc[...] = jnp.zeros_like(acc)

    def linearize(b, k):
        at = pl.ds(pl.multiple_of(b * PB, PB), PB)
        cams = [gath[k, r] for r in range(ROWS)]
        point = tuple(jnp.broadcast_to(pts_ref[i : i + 1, at], (VIEWS, PB)) for i in range(3))
        jac_cam, jac_pnt, value = jacobians(cams, point)
        residual = [value[i] - meas_ref[i, :, at] for i in range(2)]
        inv = inverse3(jac_pnt)
        grad = [
            -jnp.sum(jac_pnt[0][n] * residual[0] + jac_pnt[1][n] * residual[1], axis=0, keepdims=True)
            for n in range(3)
        ]
        moved = apply_inverse(inv, grad)
        for i in range(2):
            for r in range(ROWS):
                jc_ref[b, i * ROWS + r] = jac_cam[i][r]
            for n in range(3):
                jp_ref[b, i * 3 + n] = jac_pnt[i][n]
        for n in range(6):
            inv_ref[b, n : n + 1, :] = inv[n]
        for n in range(3):
            grad_ref[b, n : n + 1, :] = grad[n]
        left = [-residual[i] - dot3(jac_pnt[i], moved) for i in range(2)]
        squares = [jac_cam[0][r] * jac_cam[0][r] + jac_cam[1][r] * jac_cam[1][r] for r in range(ROWS)]
        scatter(b, k, squares + [jac_cam[0][r] * left[0] + jac_cam[1][r] * left[1] for r in range(ROWS)], acc)

    def linearize_pair(pair, _):
        for k in range(2):
            gather(2 * pair + k, k, 3)
        for k in range(2):
            linearize(2 * pair + k, k)
        return 0

    lax.fori_loop(0, NB // 2, linearize_pair, 0)
    send_collect(0, acc.at[0:SL])
    send_collect(1, acc.at[SL : 2 * SL])
    precond = recv_collect(0) + DAMPING
    remain = recv_collect(1)
    scaled = remain / precond
    direction = scaled
    send_deliver(2, scaled, [total(remain * scaled)])

    norm = recv_deliver(2, z_ref)[0]
    d_ref[...] = z_ref[...]

    def image_of(b, k, step):
        jac = [[jc_ref[b, i * ROWS + r] for r in range(ROWS)] for i in range(2)]
        jac_pnt = [[jp_ref[b, i * 3 + n] for n in range(3)] for i in range(2)]
        u = []
        for i in range(2):
            value = jac[i][0] * gath[k, 0]
            for r in range(1, ROWS):
                value = value + jac[i][r] * gath[k, r]
            u.append(value)
        w = [jnp.sum(jac_pnt[0][n] * u[0] + jac_pnt[1][n] * u[1], axis=0, keepdims=True) for n in range(3)]
        moved = apply_inverse([inv_ref[b, n : n + 1, :] for n in range(6)], w)
        left = [u[i] - dot3(jac_pnt[i], moved) for i in range(2)]
        return jac, u, w, moved, left

    def apply(pair, step):
        for k in range(2):
            gather(2 * pair + k, k, 2)
        for k in range(2):
            b = 2 * pair + k
            jac, _, w, _, left = image_of(b, k, step)
            for n in range(3):
                w_ref[step, b, n : n + 1, :] = w[n]
            scatter(b, k, [jac[0][r] * left[0] + jac[1][r] * left[1] for r in range(ROWS)], acc)
        return 0

    solved = None
    alphas = []
    for step in range(2):
        load_columns(d_ref[...], 2)
        acc[0:SL] = jnp.zeros((SL, 256), F32)
        lax.fori_loop(0, NB // 2, lambda pair, _: apply(pair, step), 0)
        send_collect(3 + 2 * step, acc.at[0:SL])
        image = recv_collect(3 + 2 * step) + DAMPING * direction
        quot = image / precond
        send_deliver(
            4 + 2 * step, quot,
            [total(remain * scaled), total(direction * image), total(scaled * image), total(quot * image)],
        )
        rz, dim, zim, imq = recv_deliver(4 + 2 * step, acc2)
        alpha = rz / dim
        beta = (rz - 2.0 * alpha * zim + alpha * alpha * imq) / rz
        z_ref[...] = z_ref[...] - alpha * acc2[...]
        d_ref[...] = z_ref[...] + beta * d_ref[...]
        solved = alpha * direction if step == 0 else solved + alpha * direction
        remain = remain - alpha * image
        scaled = remain / precond
        direction = scaled + beta * direction
        alphas.append(alpha)

    srcx[0:KP] = solved[0:KP]
    srcx[KP : 2 * KP] = direction[0:KP]
    srcx[2 * KP :] = solved[KP:] + lanes(direction[KP:], PIECE)
    for offset in COLUMN:
        p, _ = there(offset)
        pltpu.make_async_remote_copy(
            srcx, message(dstx, pts, 3 * KP), semx.at[0], semx.at[1], device_id=(p, cam), device_id_type=MESH
        ).start()
    pltpu.make_async_copy(srcx, message(dstx, pts, 3 * KP), semx.at[1]).start()
    load_columns(d_ref[...], 2)
    uq[...] = jnp.zeros_like(uq)

    def finish(b, k):
        _, u, _, moved, left = image_of(b, k, 2)
        uq[...] += u[0] * left[0] + u[1] * left[1]
        rest = []
        for n in range(3):
            value = grad_ref[b, n : n + 1, :]
            for step in range(2):
                value = value - alphas[step] * w_ref[step, b, n : n + 1, :]
            rest.append(value)
        rest = apply_inverse([inv_ref[b, n : n + 1, :] for n in range(6)], rest)
        at = pl.ds(pl.multiple_of(b * PB, PB), PB)
        for n in range(3):
            p0_ref[n : n + 1, at] = rest[n]
            p2_ref[n : n + 1, at] = moved[n]

    def finish_pair(pair, _):
        for k in range(2):
            gather(2 * pair + k, k, 2)
        for k in range(2):
            finish(2 * pair + k, k)
        return 0

    lax.fori_loop(0, NB // 2, finish_pair, 0)
    mine = total(uq[...]) + DAMPING * total(direction * direction)
    norm = total(remain * scaled)
    fsrc[...] = jnp.where(lane == 0, mine, jnp.where(lane == 1, norm, 0.0)).reshape(1, 1, 128)
    for offset in OFFSETS:
        p, c = there(offset)
        pltpu.make_async_remote_copy(
            fsrc.at[0], fdst.at[me], fsem.at[0], fsem.at[1], device_id=(p, c), device_id_type=MESH
        ).start()
    fdst[me] = fsrc[0]

    pltpu.make_async_copy(dstx, dstx, semx.at[1]).wait()
    for part, out in ((0, s1o), (1, d2o)):
        tail = jnp.zeros((KP, 128), F32)
        for p in range(NP):
            tail = jnp.where(lane // PIECE == p, lanes(dstx[p * 3 * KP + 2 * KP : (p + 1) * 3 * KP], PIECE * (p - part)), tail)
        for k in range(TILES):
            out[0:8, k * 128 : (k + 1) * 128] = dstx[pl.ds(part * KP + k, 8, stride=3 * KP), :]
            out[8:9, k * 128 : (k + 1) * 128] = tail[k : k + 1]

    pltpu.make_async_copy(fdst.at[pl.ds(0, ND - 1)], fdst.at[pl.ds(0, ND - 1)], fsem.at[1]).wait()
    sums = jnp.sum(fdst[...], axis=0)
    dim = jnp.sum(jnp.where(lane == 0, sums, 0.0), axis=1, keepdims=True)
    rz = jnp.sum(jnp.where(lane == 1, sums, 0.0), axis=1, keepdims=True)
    alpha = rz / dim
    cam_out[...] = s1o[...] + alpha * d2o[...]
    pnt_out[...] = p0_ref[...] - alpha * p2_ref[...]

    pltpu.make_async_copy(src0.at[pl.ds(0, 480)], dst0.at[pl.ds(0, 480)], sem0.at[0]).wait()
    for phase in range(PHASES):
        sent(phase)
    rest = pl.ds(0, 7 * 3 * KP)
    pltpu.make_async_copy(dstx.at[rest], dstx.at[rest], semx.at[0]).wait()
    pltpu.make_async_copy(fdst.at[pl.ds(0, ND - 1)], fdst.at[pl.ds(0, ND - 1)], fsem.at[0]).wait()


def shards(cam_params, points, measured, obs_slot, vis_tiles):
    vmem = pl.BlockSpec(memory_space=pltpu.VMEM)
    dma = pltpu.SemaphoreType.DMA
    return pl.pallas_call(
        kernel,
        out_shape=(
            jax.ShapeDtypeStruct(cam_params.shape, F32),
            jax.ShapeDtypeStruct(points.shape, F32),
        ),
        in_specs=[pl.BlockSpec(memory_space=pltpu.SMEM)] + [vmem] * 5,
        out_specs=(vmem, vmem),
        scratch_shapes=[
            pltpu.VMEM((TILES, 16, 128), F32),
            pltpu.VMEM((NC * 32, 128), F32),
            pltpu.VMEM((NC * 32, 128), F32),
            pltpu.VMEM((PHASES, ND * 4, 128), F32),
            pltpu.VMEM((PHASES, ND * 4, 128), F32),
            pltpu.VMEM((1, 1, 128), F32),
            pltpu.VMEM((ND, 1, 128), F32),
            pltpu.VMEM((3 * KP, 128), F32),
            pltpu.VMEM((NP * 3 * KP, 128), F32),
            pltpu.VMEM((NB, 256, OB), BF16),
            pltpu.VMEM((NB, VIEWS, PB), jnp.int32),
            pltpu.VMEM((2, 4 * SL, OB), BF16),
            pltpu.VMEM((NB, 2 * ROWS, VIEWS, PB), F32),
            pltpu.VMEM((NB, 6, VIEWS, PB), F32),
            pltpu.VMEM((NB, 8, PB), F32),
            pltpu.VMEM((NB, 8, PB), F32),
            pltpu.VMEM((2, NB, 8, PB), F32),
            pltpu.VMEM((2, 4 * ROWS, VIEWS, PB), F32),
            pltpu.VMEM((2, ROWS, VIEWS, PB), F32),
            pltpu.VMEM((3, SL, 256), BF16),
            pltpu.VMEM((2 * SL, 256), F32),
            pltpu.VMEM((SL, 256), F32),
            pltpu.VMEM((SL, 256), F32),
            pltpu.VMEM((SL, 256), F32),
            pltpu.VMEM((128, 512), BF16),
            pltpu.VMEM((512, 128), BF16),
            pltpu.VMEM((ROWS, TILES * 128), F32),
            pltpu.VMEM((ROWS, TILES * 128), F32),
            pltpu.VMEM((3, NB * PB), F32),
            pltpu.VMEM((3, NB * PB), F32),
            pltpu.VMEM((VIEWS, PB), F32),
            dma((2,)),
            dma((PHASES,)),
            dma((PHASES,)),
            dma((2,)),
            dma((2,)),
            pltpu.SemaphoreType.REGULAR,
        ],
        compiler_params=pltpu.CompilerParams(
            collective_id=0, has_side_effects=True, vmem_limit_bytes=60 << 20
        ),
    )(vis_tiles.T, vis_tiles.T, cam_params, points, measured, obs_slot)


def solution(mesh):
    placed = (
        P(None, "cam"),
        P(None, ("pts", "cam")),
        P(None, None, ("pts", "cam")),
        P(None, ("pts", "cam")),
        P(),
    )
    return jax.shard_map(
        shards,
        mesh=mesh,
        in_specs=placed,
        out_specs=(P(None, "cam"), P(None, ("pts", "cam"))),
        check_vma=False,
    )
```

```python
import functools

import jax
import jax.numpy as jnp
from jax import lax
from jax.experimental import pallas as pl
from jax.experimental.pallas import tpu as pltpu
from jax.sharding import PartitionSpec as P

MESH = pl.DeviceIdType.MESH
F32 = jnp.float32
BF16 = jnp.bfloat16
DAMPING = 0.5

NP, NC = 8, 16
ND = NP * NC
VIEWS = 8
PB = 256
NB = 8
STEP = 4
OB = VIEWS * PB
TILES = 20
KP = 24
ROWS = 9
HI = 24
SL = ROWS * HI
PIECE = 16
SCAL = 48
PHASES = 7


def hop(step):
    return min(step, 4 - step)


OFFSETS = sorted(
    [(x, k, z, y) for x in range(4) for k in range(2) for z in range(4) for y in range(4) if x or k or z or y],
    key=lambda o: -(hop(o[0]) + hop(o[2]) + hop(o[3]) + 0.3 * o[1]),
)
PLANE = [o for o in OFFSETS if not (o[0] or o[1])]
COLUMN = [o for o in OFFSETS if not (o[2] or o[3])]


def neighbours():
    pts, cam = lax.axis_index("pts"), lax.axis_index("cam")
    x, k = lax.div(pts, 2), lax.rem(pts, 2)
    z, y = lax.div(cam, 4), lax.rem(cam, 4)
    xs = [lax.rem(x + d, 4) * 2 for d in range(4)]
    ks = [k, 1 - k]
    zs = [lax.rem(z + d, 4) * 4 for d in range(4)]
    ys = [lax.rem(y + d, 4) for d in range(4)]
    columns = {(dx, dk): xs[dx] + ks[dk] for dx in range(4) for dk in range(2)}
    planes = {(dz, dy): zs[dz] + ys[dy] for dz in range(4) for dy in range(4)}
    return lambda o: (columns[o[0], o[1]], planes[o[2], o[3]])


def message(ref, index, rows):
    return ref.at[pl.ds(pl.multiple_of(index * rows, rows), rows), :]


def dot(a, b):
    return jnp.dot(a, b, preferred_element_type=F32)


def dot_nt(a, b):
    return lax.dot_general(a, b, (((1,), (1,)), ((), ())), preferred_element_type=F32)


def split(x, parts):
    out = []
    for _ in range(parts - 1):
        top = x.astype(BF16)
        out.append(top)
        x = x - top.astype(F32)
    out.append(x.astype(BF16))
    return out


def iota(shape, dim):
    return lax.broadcasted_iota(jnp.int32, shape, dim)


def total(x):
    return jnp.sum(jnp.sum(x, axis=0, keepdims=True), axis=1, keepdims=True)


def lanes(x, shift):
    shift = shift % 128
    return x if shift == 0 else pltpu.roll(x, shift, 1)


def cross(a, b):
    return (a[1] * b[2] - a[2] * b[1], a[2] * b[0] - a[0] * b[2], a[0] * b[1] - a[1] * b[0])


def dot3(a, b):
    return a[0] * b[0] + a[1] * b[1] + a[2] * b[2]


def jacobians(cam, point):
    w, t = cam[0:3], cam[3:6]
    focal, k1, k2 = cam[6:9]
    across = cross(w, point)
    twice = cross(w, across)
    turn = tuple(across[i] + twice[i] for i in range(3))
    factor = 2.0 / (1.0 + dot3(w, w))
    moved = tuple(point[i] + factor * turn[i] + t[i] for i in range(3))
    inv = 1.0 / moved[2]
    q = (moved[0] * inv, moved[1] * inv)
    s = q[0] * q[0] + q[1] * q[1]
    gain = 1.0 + k1 * s + k2 * s * s
    slope = 2.0 * focal * (k1 + 2.0 * k2 * s)
    base = focal * gain
    value = (base * q[0], base * q[1])
    mixed = slope * q[0] * q[1]
    rows = ((base + slope * q[0] * q[0], mixed), (mixed, base + slope * q[1] * q[1]))
    jac_cam, jac_pnt = [], []
    for i in range(2):
        v0, v1 = rows[i][0] * inv, rows[i][1] * inv
        v = (v0, v1, -(v0 * q[0] + v1 * q[1]))
        m = cross(v, w)
        mm = cross(m, w)
        jac_pnt.append([v[n] + factor * (m[n] + mm[n]) for n in range(3)])
        first = cross(point, tuple(v[n] + m[n] for n in range(3)))
        second = cross(across, v)
        shrink = factor * dot3(v, turn)
        rot = [factor * (first[n] + second[n] - shrink * w[n]) for n in range(3)]
        fs = focal * s * q[i]
        jac_cam.append(rot + list(v) + [gain * q[i], fs, fs * s])
    return jac_cam, jac_pnt, value


def inverse3(jac_pnt):
    n = [[None] * 3 for _ in range(3)]
    for a in range(3):
        for b in range(a, 3):
            whole = jnp.sum(jac_pnt[0][a] * jac_pnt[0][b] + jac_pnt[1][a] * jac_pnt[1][b], axis=0, keepdims=True)
            n[a][b] = n[b][a] = whole + DAMPING if a == b else whole
    c00 = n[1][1] * n[2][2] - n[1][2] * n[2][1]
    c01 = n[1][2] * n[2][0] - n[1][0] * n[2][2]
    c02 = n[1][0] * n[2][1] - n[1][1] * n[2][0]
    c11 = n[0][0] * n[2][2] - n[0][2] * n[2][0]
    c12 = n[0][1] * n[2][0] - n[0][0] * n[2][1]
    c22 = n[0][0] * n[1][1] - n[0][1] * n[1][0]
    r = 1.0 / (n[0][0] * c00 + n[0][1] * c01 + n[0][2] * c02)
    return [c00 * r, c01 * r, c02 * r, c11 * r, c12 * r, c22 * r]


def apply_inverse(inv, v):
    return (
        inv[0] * v[0] + inv[1] * v[1] + inv[2] * v[2],
        inv[1] * v[0] + inv[3] * v[1] + inv[4] * v[2],
        inv[2] * v[0] + inv[4] * v[1] + inv[5] * v[2],
    )


def kernel(
    vis_s, vis_v, cam_ref, pts_ref, meas_ref, slot_ref,
    cam_out, pnt_out,
    camt, src0, dst0, src, dst, fsrc, fdst, srcx, dstx,
    hot, hid_ref, t_ref, jc_ref, jp_ref, inv_ref, grad_ref, w_ref, terms_ref,
    gath, cols, acc, acc2, z_ref, d_ref, sel, selt, s1o, d2o, p0_ref, p2_ref, uq,
    sem0, sends, recvs, fsem, semx, ready,
):
    pts, cam = lax.axis_index("pts"), lax.axis_index("cam")
    me = pts * NC + cam
    there = neighbours()

    barrier = pltpu.get_barrier_semaphore()
    for offset in PLANE + COLUMN:
        pl.semaphore_signal(barrier, inc=1, device_id=there(offset), device_id_type=MESH)

    for k in range(TILES):
        camt[k, 0:9, :] = cam_ref[:, k * 128 : (k + 1) * 128]
    for c in range(NC):
        for j in range(3):
            one = camt[jnp.clip(vis_s[3 * cam + j, pts * NC + c] - TILES * cam, 0, TILES - 1)]
            src0[c * 32 + j * 8 : c * 32 + j * 8 + 8, :] = one[0:8]
            src0[c * 32 + 24 + j : c * 32 + 25 + j, :] = one[8:9]

    def build(b, _):
        slot = slot_ref[:, pl.ds(pl.multiple_of(b * PB, PB), PB)]
        place = slot // 128
        shard = (place * 171) // 512
        own = place - 3 * shard
        half = shard // 8
        hid_ref[b] = own * 8 + shard - 8 * half
        low = half * 128 + slot - 128 * place
        for v in range(VIEWS):
            row = jnp.broadcast_to(low[v : v + 1, :], (256, PB))
            hot[b, :, v * PB : (v + 1) * PB] = (row == iota((256, PB), 0)).astype(F32).astype(BF16)
        return 0

    lax.fori_loop(0, NB, build, 0)

    spread_rows = []
    for t in range(3):
        row = (vis_v[pl.ds(3 * cam + t, 1), :] - TILES * cam).astype(F32)
        row = jnp.broadcast_to(row, (8, 128)).astype(BF16)
        put = ((iota((128, 512), 1) // 4) == iota((128, 512), 0)).astype(F32).astype(BF16)
        spread_rows.append(dot(row, put)[0:1, :])
    quarter = iota((1, 512), 1) % 4
    index = jnp.where(quarter == 0, spread_rows[0], jnp.where(quarter == 1, spread_rows[1], spread_rows[2]))
    index = jnp.where(quarter == 3, -1.0, index)
    tile_no = iota((KP, 512), 0).astype(F32)
    blocks = [(jnp.broadcast_to(index, (KP, 512)) == tile_no).astype(F32)]
    for t in range(3):
        this = jnp.where(quarter == 3, spread_rows[t], -1.0)
        blocks.append((jnp.broadcast_to(this, (KP, 512)) == tile_no).astype(F32))
    blocks.append(jnp.zeros((128 - 4 * KP, 512), F32))
    pick = jnp.concatenate(blocks, axis=0)
    sel[...] = pick.astype(BF16)
    selt[...] = pick.T.astype(BF16)

    pl.semaphore_wait(barrier, len(PLANE) + len(COLUMN))
    for offset in COLUMN:
        pl.semaphore_signal(ready, inc=1, device_id=there(offset), device_id_type=MESH)
    for offset in PLANE:
        _, c = there(offset)
        pltpu.make_async_remote_copy(
            message(src0, c, 32), message(dst0, cam, 32), sem0.at[0], sem0.at[1],
            device_id=(pts, c), device_id_type=MESH,
        ).start()
    pltpu.make_async_copy(message(src0, cam, 32), message(dst0, cam, 32), sem0.at[1]).start()
    pltpu.make_async_copy(src0, dst0, sem0.at[1]).wait()
    pl.semaphore_wait(ready, len(COLUMN))

    def send(phase):
        for offset in OFFSETS:
            p, c = there(offset)
            to = p * NC + c
            pltpu.make_async_remote_copy(
                message(src.at[phase], to, 4), message(dst.at[phase], me, 4), sends.at[phase], recvs.at[phase],
                device_id=(p, c), device_id_type=MESH,
            ).start()
        pltpu.make_async_copy(message(src.at[phase], me, 4), message(dst.at[phase], me, 4), recvs.at[phase]).start()

    def arrived(phase):
        pltpu.make_async_copy(src.at[phase], dst.at[phase], recvs.at[phase]).wait()

    def sent(phase):
        rows = pl.ds(0, 4 * ND - 4)
        pltpu.make_async_copy(src.at[phase, rows], dst.at[phase, rows], sends.at[phase]).wait()

    lane = iota((1, 128), 1)

    def send_collect(phase, from_ref):
        for r in range(8):
            for j in range(3):
                for half in range(2):
                    src[phase, pl.ds(r * 64 + half * 32 + j, 8, stride=4), :] = from_ref[
                        r * HI + j * 8 : r * HI + j * 8 + 8, half * 128 : half * 128 + 128
                    ]
        for half in range(2):
            last = [
                from_ref[8 * HI + j * 8 : 8 * HI + j * 8 + 8, half * 128 : half * 128 + 128] for j in range(3)
            ]
            for p in range(NP):
                row = jnp.zeros((8, 128), F32)
                for j in range(3):
                    row = jnp.where(lane // PIECE == j, lanes(last[j], PIECE * (j - p)), row)
                src[phase, pl.ds(p * 64 + half * 32 + 3, 8, stride=4), :] = row
        send(phase)

    def recv_collect(phase):
        arrived(phase)
        got = sum(dot(sel[...], part) for part in split(dst[phase], 3))
        row8 = sum(lanes(got[KP * (t + 1) : KP * (t + 2)], -PIECE * t) for t in range(3))
        row8 = jnp.where(lane < PIECE, row8, 0.0)
        return jnp.concatenate([got[0:KP], row8], axis=0)

    def send_deliver(phase, own, dots):
        rows = [own[0:KP]] + [lanes(own[KP:], PIECE * t) for t in range(3)]
        rows.append(jnp.zeros((128 - 4 * KP, 128), F32))
        stacked = jnp.concatenate(rows, axis=0)
        out = sum(dot(selt[...], part) for part in split(stacked, 3))
        note = jnp.zeros((1, 128), F32)
        for i, value in enumerate(dots):
            note = jnp.where(lane == SCAL + i, value, note)
        out = out + jnp.where(iota((512, 128), 0) % 4 == 3, note, 0.0)
        src[phase] = out
        send(phase)

    def recv_deliver(phase, to_ref):
        arrived(phase)
        notes = jnp.zeros((8, 128), F32)
        for half in range(2):
            for r in range(8):
                for j in range(3):
                    to_ref[r * HI + j * 8 : r * HI + j * 8 + 8, half * 128 : half * 128 + 128] = dst[
                        phase, pl.ds(r * 64 + half * 32 + j, 8, stride=4), :
                    ]
            last = [jnp.zeros((8, 128), F32)] * 3
            for p in range(NP):
                row = dst[phase, pl.ds(p * 64 + half * 32 + 3, 8, stride=4), :]
                notes = notes + row
                for j in range(3):
                    last[j] = jnp.where(lane // PIECE == p, lanes(row, PIECE * (p - j)), last[j])
            for j in range(3):
                to_ref[8 * HI + j * 8 : 8 * HI + j * 8 + 8, half * 128 : half * 128 + 128] = last[j]
        notes = jnp.sum(notes, axis=0, keepdims=True)
        return [jnp.sum(jnp.where(lane == SCAL + i, notes, 0.0), axis=1, keepdims=True) for i in range(4)]

    def load_columns(x, parts):
        for i, part in enumerate(split(x, parts)):
            cols[i] = part

    def gather(b, k, parts):
        hid = hid_ref[b]
        for v in range(VIEWS):
            column = hot[b, :, v * PB : (v + 1) * PB]
            found = sum(dot(cols[i], column) for i in range(parts))
            mask = jnp.broadcast_to(hid[v : v + 1, :], (HI, PB)) == iota((HI, PB), 0)
            for r in range(ROWS):
                piece = found[r * HI : (r + 1) * HI]
                gath[k, r, v : v + 1, :] = jnp.sum(jnp.where(mask, piece, 0.0), axis=0, keepdims=True)

    def scatter(b, k, terms, to_ref):
        hid = hid_ref[b]
        count = len(terms)
        for r in range(count):
            top = terms[r].astype(BF16).astype(F32)
            terms_ref[k, r] = top
            terms_ref[k, count + r] = terms[r] - top
        for v in range(VIEWS):
            mask = jnp.broadcast_to(hid[v : v + 1, :], (HI, PB)) == iota((HI, PB), 0)
            for r in range(2 * count):
                row = jnp.broadcast_to(terms_ref[k, r, v : v + 1, :], (HI, PB))
                t_ref[k, r * HI : (r + 1) * HI, v * PB : (v + 1) * PB] = jnp.where(mask, row, 0.0).astype(BF16)
        both = dot_nt(t_ref[k, 0 : 2 * count * HI], hot[b])
        to_ref[0 : count * HI] += both[0 : count * HI] + both[count * HI :]

    for half in range(2):
        for j in range(3):
            for r in range(8):
                d_ref[r * HI + j * 8 : r * HI + j * 8 + 8, half * 128 : half * 128 + 128] = dst0[
                    pl.ds(half * 256 + j * 8 + r, 8, stride=32), :
                ]
            d_ref[8 * HI + j * 8 : 8 * HI + j * 8 + 8, half * 128 : half * 128 + 128] = dst0[
                pl.ds(half * 256 + 24 + j, 8, stride=32), :
            ]
    load_columns(d_ref[...], 3)
    acc[...] = jnp.zeros_like(acc)

    def linearize(b, k):
        at = pl.ds(pl.multiple_of(b * PB, PB), PB)
        cams = [gath[k, r] for r in range(ROWS)]
        point = tuple(jnp.broadcast_to(pts_ref[i : i + 1, at], (VIEWS, PB)) for i in range(3))
        jac_cam, jac_pnt, value = jacobians(cams, point)
        residual = [value[i] - meas_ref[i, :, at] for i in range(2)]
        inv = inverse3(jac_pnt)
        grad = [
            -jnp.sum(jac_pnt[0][n] * residual[0] + jac_pnt[1][n] * residual[1], axis=0, keepdims=True)
            for n in range(3)
        ]
        moved = apply_inverse(inv, grad)
        for i in range(2):
            for r in range(ROWS):
                jc_ref[b, i * ROWS + r] = jac_cam[i][r]
            for n in range(3):
                jp_ref[b, i * 3 + n] = jac_pnt[i][n]
        for n in range(6):
            inv_ref[b, n : n + 1, :] = inv[n]
        for n in range(3):
            grad_ref[b, n : n + 1, :] = grad[n]
        left = [-residual[i] - dot3(jac_pnt[i], moved) for i in range(2)]
        squares = [jac_cam[0][r] * jac_cam[0][r] + jac_cam[1][r] * jac_cam[1][r] for r in range(ROWS)]
        scatter(b, k, squares + [jac_cam[0][r] * left[0] + jac_cam[1][r] * left[1] for r in range(ROWS)], acc)

    def linearize_group(group, _):
        for k in range(STEP):
            gather(STEP * group + k, k, 3)
        for k in range(STEP):
            linearize(STEP * group + k, k)
        return 0

    lax.fori_loop(0, NB // STEP, linearize_group, 0)
    send_collect(0, acc.at[0:SL])
    send_collect(1, acc.at[SL : 2 * SL])
    precond = recv_collect(0) + DAMPING
    remain = recv_collect(1)
    scaled = remain / precond
    direction = scaled
    send_deliver(2, scaled, [total(remain * scaled)])

    norm = recv_deliver(2, z_ref)[0]
    d_ref[...] = z_ref[...]

    def image_of(b, k, step):
        jac = [[jc_ref[b, i * ROWS + r] for r in range(ROWS)] for i in range(2)]
        jac_pnt = [[jp_ref[b, i * 3 + n] for n in range(3)] for i in range(2)]
        u = []
        for i in range(2):
            value = jac[i][0] * gath[k, 0]
            for r in range(1, ROWS):
                value = value + jac[i][r] * gath[k, r]
            u.append(value)
        w = [jnp.sum(jac_pnt[0][n] * u[0] + jac_pnt[1][n] * u[1], axis=0, keepdims=True) for n in range(3)]
        moved = apply_inverse([inv_ref[b, n : n + 1, :] for n in range(6)], w)
        left = [u[i] - dot3(jac_pnt[i], moved) for i in range(2)]
        return jac, u, w, moved, left

    def apply(group, step):
        for k in range(STEP):
            gather(STEP * group + k, k, 2)
        for k in range(STEP):
            b = STEP * group + k
            jac, _, w, _, left = image_of(b, k, step)
            for n in range(3):
                w_ref[step, b, n : n + 1, :] = w[n]
            scatter(b, k, [jac[0][r] * left[0] + jac[1][r] * left[1] for r in range(ROWS)], acc)
        return 0

    solved = None
    alphas = []
    for step in range(2):
        load_columns(d_ref[...], 2)
        acc[0:SL] = jnp.zeros((SL, 256), F32)
        lax.fori_loop(0, NB // STEP, lambda group, _: apply(group, step), 0)
        send_collect(3 + 2 * step, acc.at[0:SL])
        image = recv_collect(3 + 2 * step) + DAMPING * direction
        quot = image / precond
        send_deliver(
            4 + 2 * step, quot,
            [total(remain * scaled), total(direction * image), total(scaled * image), total(quot * image)],
        )
        rz, dim, zim, imq = recv_deliver(4 + 2 * step, acc2)
        alpha = rz / dim
        beta = (rz - 2.0 * alpha * zim + alpha * alpha * imq) / rz
        z_ref[...] = z_ref[...] - alpha * acc2[...]
        d_ref[...] = z_ref[...] + beta * d_ref[...]
        solved = alpha * direction if step == 0 else solved + alpha * direction
        remain = remain - alpha * image
        scaled = remain / precond
        direction = scaled + beta * direction
        alphas.append(alpha)

    srcx[0:KP] = solved[0:KP]
    srcx[KP : 2 * KP] = direction[0:KP]
    srcx[2 * KP :] = solved[KP:] + lanes(direction[KP:], PIECE)
    for offset in COLUMN:
        p, _ = there(offset)
        pltpu.make_async_remote_copy(
            srcx, message(dstx, pts, 3 * KP), semx.at[0], semx.at[1], device_id=(p, cam), device_id_type=MESH
        ).start()
    pltpu.make_async_copy(srcx, message(dstx, pts, 3 * KP), semx.at[1]).start()
    load_columns(d_ref[...], 2)
    uq[...] = jnp.zeros_like(uq)

    def finish(b, k):
        _, u, _, moved, left = image_of(b, k, 2)
        uq[...] += u[0] * left[0] + u[1] * left[1]
        rest = []
        for n in range(3):
            value = grad_ref[b, n : n + 1, :]
            for step in range(2):
                value = value - alphas[step] * w_ref[step, b, n : n + 1, :]
            rest.append(value)
        rest = apply_inverse([inv_ref[b, n : n + 1, :] for n in range(6)], rest)
        at = pl.ds(pl.multiple_of(b * PB, PB), PB)
        for n in range(3):
            p0_ref[n : n + 1, at] = rest[n]
            p2_ref[n : n + 1, at] = moved[n]

    def finish_group(group, _):
        for k in range(STEP):
            gather(STEP * group + k, k, 2)
        for k in range(STEP):
            finish(STEP * group + k, k)
        return 0

    lax.fori_loop(0, NB // STEP, finish_group, 0)
    mine = total(uq[...]) + DAMPING * total(direction * direction)
    norm = total(remain * scaled)
    fsrc[...] = jnp.where(lane == 0, mine, jnp.where(lane == 1, norm, 0.0)).reshape(1, 1, 128)
    for offset in OFFSETS:
        p, c = there(offset)
        pltpu.make_async_remote_copy(
            fsrc.at[0], fdst.at[me], fsem.at[0], fsem.at[1], device_id=(p, c), device_id_type=MESH
        ).start()
    fdst[me] = fsrc[0]

    pltpu.make_async_copy(dstx, dstx, semx.at[1]).wait()
    for part, out in ((0, s1o), (1, d2o)):
        tail = jnp.zeros((KP, 128), F32)
        for p in range(NP):
            tail = jnp.where(lane // PIECE == p, lanes(dstx[p * 3 * KP + 2 * KP : (p + 1) * 3 * KP], PIECE * (p - part)), tail)
        for k in range(TILES):
            out[0:8, k * 128 : (k + 1) * 128] = dstx[pl.ds(part * KP + k, 8, stride=3 * KP), :]
            out[8:9, k * 128 : (k + 1) * 128] = tail[k : k + 1]

    pltpu.make_async_copy(fdst.at[pl.ds(0, ND - 1)], fdst.at[pl.ds(0, ND - 1)], fsem.at[1]).wait()
    sums = jnp.sum(fdst[...], axis=0)
    dim = jnp.sum(jnp.where(lane == 0, sums, 0.0), axis=1, keepdims=True)
    rz = jnp.sum(jnp.where(lane == 1, sums, 0.0), axis=1, keepdims=True)
    alpha = rz / dim
    cam_out[...] = s1o[...] + alpha * d2o[...]
    pnt_out[...] = p0_ref[...] - alpha * p2_ref[...]

    pltpu.make_async_copy(src0.at[pl.ds(0, 480)], dst0.at[pl.ds(0, 480)], sem0.at[0]).wait()
    for phase in range(PHASES):
        sent(phase)
    rest = pl.ds(0, 7 * 3 * KP)
    pltpu.make_async_copy(dstx.at[rest], dstx.at[rest], semx.at[0]).wait()
    pltpu.make_async_copy(fdst.at[pl.ds(0, ND - 1)], fdst.at[pl.ds(0, ND - 1)], fsem.at[0]).wait()


def shards(cam_params, points, measured, obs_slot, vis_tiles):
    vmem = pl.BlockSpec(memory_space=pltpu.VMEM)
    dma = pltpu.SemaphoreType.DMA
    return pl.pallas_call(
        kernel,
        out_shape=(
            jax.ShapeDtypeStruct(cam_params.shape, F32),
            jax.ShapeDtypeStruct(points.shape, F32),
        ),
        in_specs=[pl.BlockSpec(memory_space=pltpu.SMEM)] + [vmem] * 5,
        out_specs=(vmem, vmem),
        scratch_shapes=[
            pltpu.VMEM((TILES, 16, 128), F32),
            pltpu.VMEM((NC * 32, 128), F32),
            pltpu.VMEM((NC * 32, 128), F32),
            pltpu.VMEM((PHASES, ND * 4, 128), F32),
            pltpu.VMEM((PHASES, ND * 4, 128), F32),
            pltpu.VMEM((1, 1, 128), F32),
            pltpu.VMEM((ND, 1, 128), F32),
            pltpu.VMEM((3 * KP, 128), F32),
            pltpu.VMEM((NP * 3 * KP, 128), F32),
            pltpu.VMEM((NB, 256, OB), BF16),
            pltpu.VMEM((NB, VIEWS, PB), jnp.int32),
            pltpu.VMEM((STEP, 4 * SL, OB), BF16),
            pltpu.VMEM((NB, 2 * ROWS, VIEWS, PB), F32),
            pltpu.VMEM((NB, 6, VIEWS, PB), F32),
            pltpu.VMEM((NB, 8, PB), F32),
            pltpu.VMEM((NB, 8, PB), F32),
            pltpu.VMEM((2, NB, 8, PB), F32),
            pltpu.VMEM((STEP, 4 * ROWS, VIEWS, PB), F32),
            pltpu.VMEM((STEP, ROWS, VIEWS, PB), F32),
            pltpu.VMEM((3, SL, 256), BF16),
            pltpu.VMEM((2 * SL, 256), F32),
            pltpu.VMEM((SL, 256), F32),
            pltpu.VMEM((SL, 256), F32),
            pltpu.VMEM((SL, 256), F32),
            pltpu.VMEM((128, 512), BF16),
            pltpu.VMEM((512, 128), BF16),
            pltpu.VMEM((ROWS, TILES * 128), F32),
            pltpu.VMEM((ROWS, TILES * 128), F32),
            pltpu.VMEM((3, NB * PB), F32),
            pltpu.VMEM((3, NB * PB), F32),
            pltpu.VMEM((VIEWS, PB), F32),
            dma((2,)),
            dma((PHASES,)),
            dma((PHASES,)),
            dma((2,)),
            dma((2,)),
            pltpu.SemaphoreType.REGULAR,
        ],
        compiler_params=pltpu.CompilerParams(
            collective_id=0, has_side_effects=True, vmem_limit_bytes=60 << 20
        ),
    )(vis_tiles.T, vis_tiles.T, cam_params, points, measured, obs_slot)


def solution(mesh):
    placed = (
        P(None, "cam"),
        P(None, ("pts", "cam")),
        P(None, None, ("pts", "cam")),
        P(None, ("pts", "cam")),
        P(),
    )
    return jax.shard_map(
        shards,
        mesh=mesh,
        in_specs=placed,
        out_specs=(P(None, "cam"), P(None, ("pts", "cam"))),
        check_vma=False,
    )
```

```python
import functools

import jax
import jax.numpy as jnp
from jax import lax
from jax.experimental import pallas as pl
from jax.experimental.pallas import tpu as pltpu
from jax.sharding import PartitionSpec as P

MESH = pl.DeviceIdType.MESH
F32 = jnp.float32
BF16 = jnp.bfloat16
DAMPING = 0.5

NP, NC = 8, 16
ND = NP * NC
VIEWS = 8
PB = 256
NB = 8
STEP = 4
OB = VIEWS * PB
TILES = 20
KP = 24
ROWS = 9
HI = 24
SL = ROWS * HI
PIECE = 16
SCAL = 48
PHASES = 7


def hop(step):
    return min(step, 4 - step)


OFFSETS = sorted(
    [(x, k, z, y) for x in range(4) for k in range(2) for z in range(4) for y in range(4) if x or k or z or y],
    key=lambda o: -(hop(o[0]) + hop(o[2]) + hop(o[3]) + 0.3 * o[1]),
)
PLANE = [o for o in OFFSETS if not (o[0] or o[1])]
COLUMN = [o for o in OFFSETS if not (o[2] or o[3])]


def neighbours():
    pts, cam = lax.axis_index("pts"), lax.axis_index("cam")
    x, k = lax.div(pts, 2), lax.rem(pts, 2)
    z, y = lax.div(cam, 4), lax.rem(cam, 4)
    xs = [lax.rem(x + d, 4) * 2 for d in range(4)]
    ks = [k, 1 - k]
    zs = [lax.rem(z + d, 4) * 4 for d in range(4)]
    ys = [lax.rem(y + d, 4) for d in range(4)]
    columns = {(dx, dk): xs[dx] + ks[dk] for dx in range(4) for dk in range(2)}
    planes = {(dz, dy): zs[dz] + ys[dy] for dz in range(4) for dy in range(4)}
    return lambda o: (columns[o[0], o[1]], planes[o[2], o[3]])


def message(ref, index, rows):
    return ref.at[pl.ds(pl.multiple_of(index * rows, rows), rows), :]


def dot(a, b):
    return jnp.dot(a, b, preferred_element_type=F32)


def dot_nt(a, b):
    return lax.dot_general(a, b, (((1,), (1,)), ((), ())), preferred_element_type=F32)


def split(x, parts):
    out = []
    for _ in range(parts - 1):
        top = x.astype(BF16)
        out.append(top)
        x = x - top.astype(F32)
    out.append(x.astype(BF16))
    return out


def iota(shape, dim):
    return lax.broadcasted_iota(jnp.int32, shape, dim)


def total(x):
    return jnp.sum(jnp.sum(x, axis=0, keepdims=True), axis=1, keepdims=True)


def lanes(x, shift):
    shift = shift % 128
    return x if shift == 0 else pltpu.roll(x, shift, 1)


def cross(a, b):
    return (a[1] * b[2] - a[2] * b[1], a[2] * b[0] - a[0] * b[2], a[0] * b[1] - a[1] * b[0])


def dot3(a, b):
    return a[0] * b[0] + a[1] * b[1] + a[2] * b[2]


def jacobians(cam, point):
    w, t = cam[0:3], cam[3:6]
    focal, k1, k2 = cam[6:9]
    across = cross(w, point)
    twice = cross(w, across)
    turn = tuple(across[i] + twice[i] for i in range(3))
    factor = 2.0 / (1.0 + dot3(w, w))
    moved = tuple(point[i] + factor * turn[i] + t[i] for i in range(3))
    inv = 1.0 / moved[2]
    q = (moved[0] * inv, moved[1] * inv)
    s = q[0] * q[0] + q[1] * q[1]
    gain = 1.0 + k1 * s + k2 * s * s
    slope = 2.0 * focal * (k1 + 2.0 * k2 * s)
    base = focal * gain
    value = (base * q[0], base * q[1])
    mixed = slope * q[0] * q[1]
    rows = ((base + slope * q[0] * q[0], mixed), (mixed, base + slope * q[1] * q[1]))
    jac_cam, jac_pnt = [], []
    for i in range(2):
        v0, v1 = rows[i][0] * inv, rows[i][1] * inv
        v = (v0, v1, -(v0 * q[0] + v1 * q[1]))
        m = cross(v, w)
        mm = cross(m, w)
        jac_pnt.append([v[n] + factor * (m[n] + mm[n]) for n in range(3)])
        first = cross(point, tuple(v[n] + m[n] for n in range(3)))
        second = cross(across, v)
        shrink = factor * dot3(v, turn)
        rot = [factor * (first[n] + second[n] - shrink * w[n]) for n in range(3)]
        fs = focal * s * q[i]
        jac_cam.append(rot + list(v) + [gain * q[i], fs, fs * s])
    return jac_cam, jac_pnt, value


def inverse3(jac_pnt):
    n = [[None] * 3 for _ in range(3)]
    for a in range(3):
        for b in range(a, 3):
            whole = jnp.sum(jac_pnt[0][a] * jac_pnt[0][b] + jac_pnt[1][a] * jac_pnt[1][b], axis=0, keepdims=True)
            n[a][b] = n[b][a] = whole + DAMPING if a == b else whole
    c00 = n[1][1] * n[2][2] - n[1][2] * n[2][1]
    c01 = n[1][2] * n[2][0] - n[1][0] * n[2][2]
    c02 = n[1][0] * n[2][1] - n[1][1] * n[2][0]
    c11 = n[0][0] * n[2][2] - n[0][2] * n[2][0]
    c12 = n[0][1] * n[2][0] - n[0][0] * n[2][1]
    c22 = n[0][0] * n[1][1] - n[0][1] * n[1][0]
    r = 1.0 / (n[0][0] * c00 + n[0][1] * c01 + n[0][2] * c02)
    return [c00 * r, c01 * r, c02 * r, c11 * r, c12 * r, c22 * r]


def apply_inverse(inv, v):
    return (
        inv[0] * v[0] + inv[1] * v[1] + inv[2] * v[2],
        inv[1] * v[0] + inv[3] * v[1] + inv[4] * v[2],
        inv[2] * v[0] + inv[4] * v[1] + inv[5] * v[2],
    )


def kernel(
    vis_h, cam_h, pts_h, meas_h, slot_h,
    cam_out, pnt_out,
    vis_s, vis_v, cam_ref, pts_ref, meas_ref, slot_ref,
    camt, src0, dst0, src, dst, fsrc, fdst, srcx, dstx,
    hot, hid_ref, t_ref, jc_ref, jp_ref, inv_ref, grad_ref, w_ref, terms_ref,
    gath, cols, acc, acc2, z_ref, d_ref, sel, selt, s1o, d2o, p0_ref, p2_ref, uq,
    insems, sem0, sends, recvs, fsem, semx, ready,
):
    pts, cam = lax.axis_index("pts"), lax.axis_index("cam")
    me = pts * NC + cam
    there = neighbours()

    barrier = pltpu.get_barrier_semaphore()
    for offset in PLANE + COLUMN:
        pl.semaphore_signal(barrier, inc=1, device_id=there(offset), device_id_type=MESH)

    pairs = ((vis_h, vis_s), (cam_h, cam_ref), (slot_h, slot_ref), (vis_h, vis_v), (pts_h, pts_ref), (meas_h, meas_ref))
    loads = [pltpu.make_async_copy(a, b, insems.at[i]) for i, (a, b) in enumerate(pairs)]
    for load in loads:
        load.start()

    loads[0].wait()
    loads[1].wait()
    for k in range(TILES):
        camt[k, 0:9, :] = cam_ref[:, k * 128 : (k + 1) * 128]
    for c in range(NC):
        for j in range(3):
            one = camt[jnp.clip(vis_s[3 * cam + j, pts * NC + c] - TILES * cam, 0, TILES - 1)]
            src0[c * 32 + j * 8 : c * 32 + j * 8 + 8, :] = one[0:8]
            src0[c * 32 + 24 + j : c * 32 + 25 + j, :] = one[8:9]

    def build(b, _):
        slot = slot_ref[:, pl.ds(pl.multiple_of(b * PB, PB), PB)]
        place = slot // 128
        shard = (place * 171) // 512
        own = place - 3 * shard
        half = shard // 8
        hid_ref[b] = own * 8 + shard - 8 * half
        low = half * 128 + slot - 128 * place
        for v in range(VIEWS):
            row = jnp.broadcast_to(low[v : v + 1, :], (256, PB))
            hot[b, :, v * PB : (v + 1) * PB] = (row == iota((256, PB), 0)).astype(F32).astype(BF16)
        return 0

    loads[2].wait()
    lax.fori_loop(0, NB, build, 0)
    for load in loads[3:]:
        load.wait()

    spread_rows = []
    for t in range(3):
        row = (vis_v[pl.ds(3 * cam + t, 1), :] - TILES * cam).astype(F32)
        row = jnp.broadcast_to(row, (8, 128)).astype(BF16)
        put = ((iota((128, 512), 1) // 4) == iota((128, 512), 0)).astype(F32).astype(BF16)
        spread_rows.append(dot(row, put)[0:1, :])
    quarter = iota((1, 512), 1) % 4
    index = jnp.where(quarter == 0, spread_rows[0], jnp.where(quarter == 1, spread_rows[1], spread_rows[2]))
    index = jnp.where(quarter == 3, -1.0, index)
    tile_no = iota((KP, 512), 0).astype(F32)
    blocks = [(jnp.broadcast_to(index, (KP, 512)) == tile_no).astype(F32)]
    for t in range(3):
        this = jnp.where(quarter == 3, spread_rows[t], -1.0)
        blocks.append((jnp.broadcast_to(this, (KP, 512)) == tile_no).astype(F32))
    blocks.append(jnp.zeros((128 - 4 * KP, 512), F32))
    pick = jnp.concatenate(blocks, axis=0)
    sel[...] = pick.astype(BF16)
    selt[...] = pick.T.astype(BF16)

    pl.semaphore_wait(barrier, len(PLANE) + len(COLUMN))
    for offset in PLANE:
        _, c = there(offset)
        pltpu.make_async_remote_copy(
            message(src0, c, 32), message(dst0, cam, 32), sem0.at[0], sem0.at[1],
            device_id=(pts, c), device_id_type=MESH,
        ).start()
    for offset in COLUMN:
        pl.semaphore_signal(ready, inc=1, device_id=there(offset), device_id_type=MESH)
    pltpu.make_async_copy(message(src0, cam, 32), message(dst0, cam, 32), sem0.at[1]).start()
    pltpu.make_async_copy(src0, dst0, sem0.at[1]).wait()
    pl.semaphore_wait(ready, len(COLUMN))

    def send(phase):
        for offset in OFFSETS:
            p, c = there(offset)
            to = p * NC + c
            pltpu.make_async_remote_copy(
                message(src.at[phase], to, 4), message(dst.at[phase], me, 4), sends.at[phase], recvs.at[phase],
                device_id=(p, c), device_id_type=MESH,
            ).start()
        pltpu.make_async_copy(message(src.at[phase], me, 4), message(dst.at[phase], me, 4), recvs.at[phase]).start()

    def arrived(phase):
        pltpu.make_async_copy(src.at[phase], dst.at[phase], recvs.at[phase]).wait()

    def sent(phase):
        rows = pl.ds(0, 4 * ND - 4)
        pltpu.make_async_copy(src.at[phase, rows], dst.at[phase, rows], sends.at[phase]).wait()

    lane = iota((1, 128), 1)

    def send_collect(phase, from_ref):
        for r in range(8):
            for j in range(3):
                for half in range(2):
                    src[phase, pl.ds(r * 64 + half * 32 + j, 8, stride=4), :] = from_ref[
                        r * HI + j * 8 : r * HI + j * 8 + 8, half * 128 : half * 128 + 128
                    ]
        for half in range(2):
            last = [
                from_ref[8 * HI + j * 8 : 8 * HI + j * 8 + 8, half * 128 : half * 128 + 128] for j in range(3)
            ]
            for p in range(NP):
                row = jnp.zeros((8, 128), F32)
                for j in range(3):
                    row = jnp.where(lane // PIECE == j, lanes(last[j], PIECE * (j - p)), row)
                src[phase, pl.ds(p * 64 + half * 32 + 3, 8, stride=4), :] = row
        send(phase)

    def recv_collect(phase):
        arrived(phase)
        got = sum(dot(sel[...], part) for part in split(dst[phase], 3))
        row8 = sum(lanes(got[KP * (t + 1) : KP * (t + 2)], -PIECE * t) for t in range(3))
        row8 = jnp.where(lane < PIECE, row8, 0.0)
        return jnp.concatenate([got[0:KP], row8], axis=0)

    def send_deliver(phase, own, dots):
        rows = [own[0:KP]] + [lanes(own[KP:], PIECE * t) for t in range(3)]
        rows.append(jnp.zeros((128 - 4 * KP, 128), F32))
        stacked = jnp.concatenate(rows, axis=0)
        out = sum(dot(selt[...], part) for part in split(stacked, 3))
        note = jnp.zeros((1, 128), F32)
        for i, value in enumerate(dots):
            note = jnp.where(lane == SCAL + i, value, note)
        out = out + jnp.where(iota((512, 128), 0) % 4 == 3, note, 0.0)
        src[phase] = out
        send(phase)

    def recv_deliver(phase, to_ref):
        arrived(phase)
        notes = jnp.zeros((8, 128), F32)
        for half in range(2):
            for r in range(8):
                for j in range(3):
                    to_ref[r * HI + j * 8 : r * HI + j * 8 + 8, half * 128 : half * 128 + 128] = dst[
                        phase, pl.ds(r * 64 + half * 32 + j, 8, stride=4), :
                    ]
            last = [jnp.zeros((8, 128), F32)] * 3
            for p in range(NP):
                row = dst[phase, pl.ds(p * 64 + half * 32 + 3, 8, stride=4), :]
                notes = notes + row
                for j in range(3):
                    last[j] = jnp.where(lane // PIECE == p, lanes(row, PIECE * (p - j)), last[j])
            for j in range(3):
                to_ref[8 * HI + j * 8 : 8 * HI + j * 8 + 8, half * 128 : half * 128 + 128] = last[j]
        notes = jnp.sum(notes, axis=0, keepdims=True)
        return [jnp.sum(jnp.where(lane == SCAL + i, notes, 0.0), axis=1, keepdims=True) for i in range(4)]

    def load_columns(x, parts):
        for i, part in enumerate(split(x, parts)):
            cols[i] = part

    def gather(b, k, parts):
        hid = hid_ref[b]
        for v in range(VIEWS):
            column = hot[b, :, v * PB : (v + 1) * PB]
            found = sum(dot(cols[i], column) for i in range(parts))
            mask = jnp.broadcast_to(hid[v : v + 1, :], (HI, PB)) == iota((HI, PB), 0)
            for r in range(ROWS):
                piece = found[r * HI : (r + 1) * HI]
                gath[k, r, v : v + 1, :] = jnp.sum(jnp.where(mask, piece, 0.0), axis=0, keepdims=True)

    def scatter(b, k, terms, to_ref):
        hid = hid_ref[b]
        count = len(terms)
        for r in range(count):
            top = terms[r].astype(BF16).astype(F32)
            terms_ref[k, r] = top
            terms_ref[k, count + r] = terms[r] - top
        for v in range(VIEWS):
            mask = jnp.broadcast_to(hid[v : v + 1, :], (HI, PB)) == iota((HI, PB), 0)
            for r in range(2 * count):
                row = jnp.broadcast_to(terms_ref[k, r, v : v + 1, :], (HI, PB))
                t_ref[k, r * HI : (r + 1) * HI, v * PB : (v + 1) * PB] = jnp.where(mask, row, 0.0).astype(BF16)
        both = dot_nt(t_ref[k, 0 : 2 * count * HI], hot[b])
        to_ref[0 : count * HI] += both[0 : count * HI] + both[count * HI :]

    for half in range(2):
        for j in range(3):
            for r in range(8):
                d_ref[r * HI + j * 8 : r * HI + j * 8 + 8, half * 128 : half * 128 + 128] = dst0[
                    pl.ds(half * 256 + j * 8 + r, 8, stride=32), :
                ]
            d_ref[8 * HI + j * 8 : 8 * HI + j * 8 + 8, half * 128 : half * 128 + 128] = dst0[
                pl.ds(half * 256 + 24 + j, 8, stride=32), :
            ]
    load_columns(d_ref[...], 3)
    acc[...] = jnp.zeros_like(acc)

    def linearize(b, k):
        at = pl.ds(pl.multiple_of(b * PB, PB), PB)
        cams = [gath[k, r] for r in range(ROWS)]
        point = tuple(jnp.broadcast_to(pts_ref[i : i + 1, at], (VIEWS, PB)) for i in range(3))
        jac_cam, jac_pnt, value = jacobians(cams, point)
        residual = [value[i] - meas_ref[i, :, at] for i in range(2)]
        inv = inverse3(jac_pnt)
        grad = [
            -jnp.sum(jac_pnt[0][n] * residual[0] + jac_pnt[1][n] * residual[1], axis=0, keepdims=True)
            for n in range(3)
        ]
        moved = apply_inverse(inv, grad)
        for i in range(2):
            for r in range(ROWS):
                jc_ref[b, i * ROWS + r] = jac_cam[i][r]
            for n in range(3):
                jp_ref[b, i * 3 + n] = jac_pnt[i][n]
        for n in range(6):
            inv_ref[b, n : n + 1, :] = inv[n]
        for n in range(3):
            grad_ref[b, n : n + 1, :] = grad[n]
        left = [-residual[i] - dot3(jac_pnt[i], moved) for i in range(2)]
        squares = [jac_cam[0][r] * jac_cam[0][r] + jac_cam[1][r] * jac_cam[1][r] for r in range(ROWS)]
        scatter(b, k, squares + [jac_cam[0][r] * left[0] + jac_cam[1][r] * left[1] for r in range(ROWS)], acc)

    def linearize_group(group, _):
        for k in range(STEP):
            gather(STEP * group + k, k, 3)
        for k in range(STEP):
            linearize(STEP * group + k, k)
        return 0

    lax.fori_loop(0, NB // STEP, linearize_group, 0)
    send_collect(0, acc.at[0:SL])
    send_collect(1, acc.at[SL : 2 * SL])
    precond = recv_collect(0) + DAMPING
    remain = recv_collect(1)
    scaled = remain / precond
    direction = scaled
    send_deliver(2, scaled, [total(remain * scaled)])

    norm = recv_deliver(2, z_ref)[0]
    d_ref[...] = z_ref[...]

    def image_of(b, k, step):
        jac = [[jc_ref[b, i * ROWS + r] for r in range(ROWS)] for i in range(2)]
        jac_pnt = [[jp_ref[b, i * 3 + n] for n in range(3)] for i in range(2)]
        u = []
        for i in range(2):
            value = jac[i][0] * gath[k, 0]
            for r in range(1, ROWS):
                value = value + jac[i][r] * gath[k, r]
            u.append(value)
        w = [jnp.sum(jac_pnt[0][n] * u[0] + jac_pnt[1][n] * u[1], axis=0, keepdims=True) for n in range(3)]
        moved = apply_inverse([inv_ref[b, n : n + 1, :] for n in range(6)], w)
        left = [u[i] - dot3(jac_pnt[i], moved) for i in range(2)]
        return jac, u, w, moved, left

    def apply(group, step):
        for k in range(STEP):
            gather(STEP * group + k, k, 2)
        for k in range(STEP):
            b = STEP * group + k
            jac, _, w, _, left = image_of(b, k, step)
            for n in range(3):
                w_ref[step, b, n : n + 1, :] = w[n]
            scatter(b, k, [jac[0][r] * left[0] + jac[1][r] * left[1] for r in range(ROWS)], acc)
        return 0

    solved = None
    alphas = []
    for step in range(2):
        load_columns(d_ref[...], 2)
        acc[0:SL] = jnp.zeros((SL, 256), F32)
        lax.fori_loop(0, NB // STEP, lambda group, _: apply(group, step), 0)
        send_collect(3 + 2 * step, acc.at[0:SL])
        image = recv_collect(3 + 2 * step) + DAMPING * direction
        quot = image / precond
        send_deliver(
            4 + 2 * step, quot,
            [total(remain * scaled), total(direction * image), total(scaled * image), total(quot * image)],
        )
        rz, dim, zim, imq = recv_deliver(4 + 2 * step, acc2)
        alpha = rz / dim
        beta = (rz - 2.0 * alpha * zim + alpha * alpha * imq) / rz
        z_ref[...] = z_ref[...] - alpha * acc2[...]
        d_ref[...] = z_ref[...] + beta * d_ref[...]
        solved = alpha * direction if step == 0 else solved + alpha * direction
        remain = remain - alpha * image
        scaled = remain / precond
        direction = scaled + beta * direction
        alphas.append(alpha)

    srcx[0:KP] = solved[0:KP]
    srcx[KP : 2 * KP] = direction[0:KP]
    srcx[2 * KP :] = solved[KP:] + lanes(direction[KP:], PIECE)
    for offset in COLUMN:
        p, _ = there(offset)
        pltpu.make_async_remote_copy(
            srcx, message(dstx, pts, 3 * KP), semx.at[0], semx.at[1], device_id=(p, cam), device_id_type=MESH
        ).start()
    pltpu.make_async_copy(srcx, message(dstx, pts, 3 * KP), semx.at[1]).start()
    load_columns(d_ref[...], 2)
    uq[...] = jnp.zeros_like(uq)

    def finish(b, k):
        _, u, _, moved, left = image_of(b, k, 2)
        uq[...] += u[0] * left[0] + u[1] * left[1]
        rest = []
        for n in range(3):
            value = grad_ref[b, n : n + 1, :]
            for step in range(2):
                value = value - alphas[step] * w_ref[step, b, n : n + 1, :]
            rest.append(value)
        rest = apply_inverse([inv_ref[b, n : n + 1, :] for n in range(6)], rest)
        at = pl.ds(pl.multiple_of(b * PB, PB), PB)
        for n in range(3):
            p0_ref[n : n + 1, at] = rest[n]
            p2_ref[n : n + 1, at] = moved[n]

    def finish_group(group, _):
        for k in range(STEP):
            gather(STEP * group + k, k, 2)
        for k in range(STEP):
            finish(STEP * group + k, k)
        return 0

    lax.fori_loop(0, NB // STEP, finish_group, 0)
    mine = total(uq[...]) + DAMPING * total(direction * direction)
    norm = total(remain * scaled)
    fsrc[...] = jnp.where(lane == 0, mine, jnp.where(lane == 1, norm, 0.0)).reshape(1, 1, 128)
    for offset in OFFSETS:
        p, c = there(offset)
        pltpu.make_async_remote_copy(
            fsrc.at[0], fdst.at[me], fsem.at[0], fsem.at[1], device_id=(p, c), device_id_type=MESH
        ).start()
    fdst[me] = fsrc[0]

    pltpu.make_async_copy(dstx, dstx, semx.at[1]).wait()
    for part, out in ((0, s1o), (1, d2o)):
        tail = jnp.zeros((KP, 128), F32)
        for p in range(NP):
            tail = jnp.where(lane // PIECE == p, lanes(dstx[p * 3 * KP + 2 * KP : (p + 1) * 3 * KP], PIECE * (p - part)), tail)
        for k in range(TILES):
            out[0:8, k * 128 : (k + 1) * 128] = dstx[pl.ds(part * KP + k, 8, stride=3 * KP), :]
            out[8:9, k * 128 : (k + 1) * 128] = tail[k : k + 1]

    pltpu.make_async_copy(fdst.at[pl.ds(0, ND - 1)], fdst.at[pl.ds(0, ND - 1)], fsem.at[1]).wait()
    sums = jnp.sum(fdst[...], axis=0)
    dim = jnp.sum(jnp.where(lane == 0, sums, 0.0), axis=1, keepdims=True)
    rz = jnp.sum(jnp.where(lane == 1, sums, 0.0), axis=1, keepdims=True)
    alpha = rz / dim
    cam_out[...] = s1o[...] + alpha * d2o[...]
    pnt_out[...] = p0_ref[...] - alpha * p2_ref[...]

    pltpu.make_async_copy(src0.at[pl.ds(0, 480)], dst0.at[pl.ds(0, 480)], sem0.at[0]).wait()
    for phase in range(PHASES):
        sent(phase)
    rest = pl.ds(0, 7 * 3 * KP)
    pltpu.make_async_copy(dstx.at[rest], dstx.at[rest], semx.at[0]).wait()
    pltpu.make_async_copy(fdst.at[pl.ds(0, ND - 1)], fdst.at[pl.ds(0, ND - 1)], fsem.at[0]).wait()


def shards(cam_params, points, measured, obs_slot, vis_tiles):
    vmem = pl.BlockSpec(memory_space=pltpu.VMEM)
    dma = pltpu.SemaphoreType.DMA
    return pl.pallas_call(
        kernel,
        out_shape=(
            jax.ShapeDtypeStruct(cam_params.shape, F32),
            jax.ShapeDtypeStruct(points.shape, F32),
        ),
        in_specs=[pl.BlockSpec(memory_space=pl.ANY)] * 5,
        out_specs=(vmem, vmem),
        scratch_shapes=[
            pltpu.SMEM(vis_tiles.shape[::-1], jnp.int32),
            pltpu.VMEM(vis_tiles.shape[::-1], jnp.int32),
            pltpu.VMEM(cam_params.shape, F32),
            pltpu.VMEM(points.shape, F32),
            pltpu.VMEM(measured.shape, F32),
            pltpu.VMEM(obs_slot.shape, jnp.int32),
            pltpu.VMEM((TILES, 16, 128), F32),
            pltpu.VMEM((NC * 32, 128), F32),
            pltpu.VMEM((NC * 32, 128), F32),
            pltpu.VMEM((PHASES, ND * 4, 128), F32),
            pltpu.VMEM((PHASES, ND * 4, 128), F32),
            pltpu.VMEM((1, 1, 128), F32),
            pltpu.VMEM((ND, 1, 128), F32),
            pltpu.VMEM((3 * KP, 128), F32),
            pltpu.VMEM((NP * 3 * KP, 128), F32),
            pltpu.VMEM((NB, 256, OB), BF16),
            pltpu.VMEM((NB, VIEWS, PB), jnp.int32),
            pltpu.VMEM((STEP, 4 * SL, OB), BF16),
            pltpu.VMEM((NB, 2 * ROWS, VIEWS, PB), F32),
            pltpu.VMEM((NB, 6, VIEWS, PB), F32),
            pltpu.VMEM((NB, 8, PB), F32),
            pltpu.VMEM((NB, 8, PB), F32),
            pltpu.VMEM((2, NB, 8, PB), F32),
            pltpu.VMEM((STEP, 4 * ROWS, VIEWS, PB), F32),
            pltpu.VMEM((STEP, ROWS, VIEWS, PB), F32),
            pltpu.VMEM((3, SL, 256), BF16),
            pltpu.VMEM((2 * SL, 256), F32),
            pltpu.VMEM((SL, 256), F32),
            pltpu.VMEM((SL, 256), F32),
            pltpu.VMEM((SL, 256), F32),
            pltpu.VMEM((128, 512), BF16),
            pltpu.VMEM((512, 128), BF16),
            pltpu.VMEM((ROWS, TILES * 128), F32),
            pltpu.VMEM((ROWS, TILES * 128), F32),
            pltpu.VMEM((3, NB * PB), F32),
            pltpu.VMEM((3, NB * PB), F32),
            pltpu.VMEM((VIEWS, PB), F32),
            dma((6,)),
            dma((2,)),
            dma((PHASES,)),
            dma((PHASES,)),
            dma((2,)),
            dma((2,)),
            pltpu.SemaphoreType.REGULAR,
        ],
        compiler_params=pltpu.CompilerParams(
            collective_id=0, has_side_effects=True, vmem_limit_bytes=60 << 20
        ),
    )(vis_tiles.T, cam_params, points, measured, obs_slot)


def solution(mesh):
    placed = (
        P(None, "cam"),
        P(None, ("pts", "cam")),
        P(None, None, ("pts", "cam")),
        P(None, ("pts", "cam")),
        P(),
    )
    return jax.shard_map(
        shards,
        mesh=mesh,
        in_specs=placed,
        out_specs=(P(None, "cam"), P(None, ("pts", "cam"))),
        check_vma=False,
    )
```

```python
import functools

import jax
import jax.numpy as jnp
from jax import lax
from jax.experimental import pallas as pl
from jax.experimental.pallas import tpu as pltpu
from jax.sharding import PartitionSpec as P

MESH = pl.DeviceIdType.MESH
F32 = jnp.float32
BF16 = jnp.bfloat16
DAMPING = 0.5

NP, NC = 8, 16
ND = NP * NC
VIEWS = 8
PB = 256
NB = 8
STEP = 4
OB = VIEWS * PB
TILES = 20
KP = 24
ROWS = 9
HI = 24
SL = ROWS * HI
PIECE = 16
SCAL = 48
PHASES = 7


def hop(step):
    return min(step, 4 - step)


OFFSETS = sorted(
    [(x, k, z, y) for x in range(4) for k in range(2) for z in range(4) for y in range(4) if x or k or z or y],
    key=lambda o: -(hop(o[0]) + hop(o[2]) + hop(o[3]) + 0.3 * o[1]),
)
PLANE = [o for o in OFFSETS if not (o[0] or o[1])]
COLUMN = [o for o in OFFSETS if not (o[2] or o[3])]


def neighbours():
    pts, cam = lax.axis_index("pts"), lax.axis_index("cam")
    x, k = lax.div(pts, 2), lax.rem(pts, 2)
    z, y = lax.div(cam, 4), lax.rem(cam, 4)
    xs = [lax.rem(x + d, 4) * 2 for d in range(4)]
    ks = [k, 1 - k]
    zs = [lax.rem(z + d, 4) * 4 for d in range(4)]
    ys = [lax.rem(y + d, 4) for d in range(4)]
    columns = {(dx, dk): xs[dx] + ks[dk] for dx in range(4) for dk in range(2)}
    planes = {(dz, dy): zs[dz] + ys[dy] for dz in range(4) for dy in range(4)}
    return lambda o: (columns[o[0], o[1]], planes[o[2], o[3]])


def message(ref, index, rows):
    return ref.at[pl.ds(pl.multiple_of(index * rows, rows), rows), :]


def dot(a, b):
    return jnp.dot(a, b, preferred_element_type=F32)


def dot_nt(a, b):
    return lax.dot_general(a, b, (((1,), (1,)), ((), ())), preferred_element_type=F32)


def split(x, parts):
    out = []
    for _ in range(parts - 1):
        top = x.astype(BF16)
        out.append(top)
        x = x - top.astype(F32)
    out.append(x.astype(BF16))
    return out


def iota(shape, dim):
    return lax.broadcasted_iota(jnp.int32, shape, dim)


def total(x):
    return jnp.sum(jnp.sum(x, axis=0, keepdims=True), axis=1, keepdims=True)


def lanes(x, shift):
    shift = shift % 128
    return x if shift == 0 else pltpu.roll(x, shift, 1)


def cross(a, b):
    return (a[1] * b[2] - a[2] * b[1], a[2] * b[0] - a[0] * b[2], a[0] * b[1] - a[1] * b[0])


def dot3(a, b):
    return a[0] * b[0] + a[1] * b[1] + a[2] * b[2]


def jacobians(cam, point):
    w, t = cam[0:3], cam[3:6]
    focal, k1, k2 = cam[6:9]
    across = cross(w, point)
    twice = cross(w, across)
    turn = tuple(across[i] + twice[i] for i in range(3))
    factor = 2.0 / (1.0 + dot3(w, w))
    moved = tuple(point[i] + factor * turn[i] + t[i] for i in range(3))
    inv = 1.0 / moved[2]
    q = (moved[0] * inv, moved[1] * inv)
    s = q[0] * q[0] + q[1] * q[1]
    gain = 1.0 + k1 * s + k2 * s * s
    slope = 2.0 * focal * (k1 + 2.0 * k2 * s)
    base = focal * gain
    value = (base * q[0], base * q[1])
    mixed = slope * q[0] * q[1]
    rows = ((base + slope * q[0] * q[0], mixed), (mixed, base + slope * q[1] * q[1]))
    jac_cam, jac_pnt = [], []
    for i in range(2):
        v0, v1 = rows[i][0] * inv, rows[i][1] * inv
        v = (v0, v1, -(v0 * q[0] + v1 * q[1]))
        m = cross(v, w)
        mm = cross(m, w)
        jac_pnt.append([v[n] + factor * (m[n] + mm[n]) for n in range(3)])
        first = cross(point, tuple(v[n] + m[n] for n in range(3)))
        second = cross(across, v)
        shrink = factor * dot3(v, turn)
        rot = [factor * (first[n] + second[n] - shrink * w[n]) for n in range(3)]
        fs = focal * s * q[i]
        jac_cam.append(rot + list(v) + [gain * q[i], fs, fs * s])
    return jac_cam, jac_pnt, value


def inverse3(jac_pnt):
    n = [[None] * 3 for _ in range(3)]
    for a in range(3):
        for b in range(a, 3):
            whole = jnp.sum(jac_pnt[0][a] * jac_pnt[0][b] + jac_pnt[1][a] * jac_pnt[1][b], axis=0, keepdims=True)
            n[a][b] = n[b][a] = whole + DAMPING if a == b else whole
    c00 = n[1][1] * n[2][2] - n[1][2] * n[2][1]
    c01 = n[1][2] * n[2][0] - n[1][0] * n[2][2]
    c02 = n[1][0] * n[2][1] - n[1][1] * n[2][0]
    c11 = n[0][0] * n[2][2] - n[0][2] * n[2][0]
    c12 = n[0][1] * n[2][0] - n[0][0] * n[2][1]
    c22 = n[0][0] * n[1][1] - n[0][1] * n[1][0]
    r = 1.0 / (n[0][0] * c00 + n[0][1] * c01 + n[0][2] * c02)
    return [c00 * r, c01 * r, c02 * r, c11 * r, c12 * r, c22 * r]


def apply_inverse(inv, v):
    return (
        inv[0] * v[0] + inv[1] * v[1] + inv[2] * v[2],
        inv[1] * v[0] + inv[3] * v[1] + inv[4] * v[2],
        inv[2] * v[0] + inv[4] * v[1] + inv[5] * v[2],
    )


def kernel(
    vis_h, cam_h, pts_h, meas_h, slot_h,
    cam_out, pnt_out,
    vis_s, vis_v, cam_ref, pts_ref, meas_ref, slot_ref,
    camt, src0, dst0, src, dst, fsrc, fdst, srcx, dstx,
    hot, hid_ref, t_ref, jc_ref, jp_ref, inv_ref, grad_ref, w_ref, terms_ref,
    gath, cols, acc, acc2, z_ref, d_ref, sel, selt, s1o, d2o, p0_ref, p2_ref, uq,
    insems, sem0, sends, recvs, fsem, semx, ready,
):
    pts, cam = lax.axis_index("pts"), lax.axis_index("cam")
    me = pts * NC + cam
    there = neighbours()

    barrier = pltpu.get_barrier_semaphore()
    for offset in PLANE + COLUMN:
        pl.semaphore_signal(barrier, inc=1, device_id=there(offset), device_id_type=MESH)

    pairs = ((vis_h, vis_s), (cam_h, cam_ref), (slot_h, slot_ref), (vis_h, vis_v), (pts_h, pts_ref), (meas_h, meas_ref))
    loads = [pltpu.make_async_copy(a, b, insems.at[i]) for i, (a, b) in enumerate(pairs)]
    for load in loads:
        load.start()

    loads[0].wait()
    loads[1].wait()
    for k in range(TILES):
        camt[k, 0:9, :] = cam_ref[:, k * 128 : (k + 1) * 128]
    for c in range(NC):
        for j in range(3):
            one = camt[jnp.clip(vis_s[3 * cam + j, pts * NC + c] - TILES * cam, 0, TILES - 1)]
            src0[c * 32 + j * 8 : c * 32 + j * 8 + 8, :] = one[0:8]
            src0[c * 32 + 24 + j : c * 32 + 25 + j, :] = one[8:9]

    def build(b, _):
        slot = slot_ref[:, pl.ds(pl.multiple_of(b * PB, PB), PB)]
        place = slot // 128
        shard = (place * 171) // 512
        own = place - 3 * shard
        half = shard // 8
        hid_ref[b] = own * 8 + shard - 8 * half
        low = half * 128 + slot - 128 * place
        for v in range(VIEWS):
            row = jnp.broadcast_to(low[v : v + 1, :], (256, PB))
            hot[b, :, v * PB : (v + 1) * PB] = (row == iota((256, PB), 0)).astype(F32).astype(BF16)
        return 0

    loads[2].wait()
    lax.fori_loop(0, NB, build, 0)
    for load in loads[3:]:
        load.wait()

    spread_rows = []
    for t in range(3):
        row = (vis_v[pl.ds(3 * cam + t, 1), :] - TILES * cam).astype(F32)
        row = jnp.broadcast_to(row, (8, 128)).astype(BF16)
        put = ((iota((128, 512), 1) // 4) == iota((128, 512), 0)).astype(F32).astype(BF16)
        spread_rows.append(dot(row, put)[0:1, :])
    quarter = iota((1, 512), 1) % 4
    index = jnp.where(quarter == 0, spread_rows[0], jnp.where(quarter == 1, spread_rows[1], spread_rows[2]))
    index = jnp.where(quarter == 3, -1.0, index)
    tile_no = iota((KP, 512), 0).astype(F32)
    blocks = [(jnp.broadcast_to(index, (KP, 512)) == tile_no).astype(F32)]
    for t in range(3):
        this = jnp.where(quarter == 3, spread_rows[t], -1.0)
        blocks.append((jnp.broadcast_to(this, (KP, 512)) == tile_no).astype(F32))
    blocks.append(jnp.zeros((128 - 4 * KP, 512), F32))
    pick = jnp.concatenate(blocks, axis=0)
    sel[...] = pick.astype(BF16)
    selt[...] = pick.T.astype(BF16)

    pl.semaphore_wait(barrier, len(PLANE) + len(COLUMN))
    for offset in PLANE:
        _, c = there(offset)
        pltpu.make_async_remote_copy(
            message(src0, c, 32), message(dst0, cam, 32), sem0.at[0], sem0.at[1],
            device_id=(pts, c), device_id_type=MESH,
        ).start()
    for offset in COLUMN:
        pl.semaphore_signal(ready, inc=1, device_id=there(offset), device_id_type=MESH)
    pltpu.make_async_copy(message(src0, cam, 32), message(dst0, cam, 32), sem0.at[1]).start()
    pltpu.make_async_copy(src0, dst0, sem0.at[1]).wait()
    pl.semaphore_wait(ready, len(COLUMN))

    def send(phase):
        for offset in OFFSETS:
            p, c = there(offset)
            to = p * NC + c
            pltpu.make_async_remote_copy(
                message(src.at[phase], to, 4), message(dst.at[phase], me, 4), sends.at[phase], recvs.at[phase],
                device_id=(p, c), device_id_type=MESH,
            ).start()
        pltpu.make_async_copy(message(src.at[phase], me, 4), message(dst.at[phase], me, 4), recvs.at[phase]).start()

    def arrived(phase):
        pltpu.make_async_copy(src.at[phase], dst.at[phase], recvs.at[phase]).wait()

    def sent(phase):
        rows = pl.ds(0, 4 * ND - 4)
        pltpu.make_async_copy(src.at[phase, rows], dst.at[phase, rows], sends.at[phase]).wait()

    lane = iota((1, 128), 1)

    def send_collect(phase, from_ref):
        for r in range(8):
            for j in range(3):
                for half in range(2):
                    src[phase, pl.ds(r * 64 + half * 32 + j, 8, stride=4), :] = from_ref[
                        r * HI + j * 8 : r * HI + j * 8 + 8, half * 128 : half * 128 + 128
                    ]
        for half in range(2):
            last = [
                from_ref[8 * HI + j * 8 : 8 * HI + j * 8 + 8, half * 128 : half * 128 + 128] for j in range(3)
            ]
            for p in range(NP):
                row = jnp.zeros((8, 128), F32)
                for j in range(3):
                    row = jnp.where(lane // PIECE == j, lanes(last[j], PIECE * (j - p)), row)
                src[phase, pl.ds(p * 64 + half * 32 + 3, 8, stride=4), :] = row
        send(phase)

    def recv_collect(phase):
        arrived(phase)
        got = sum(dot(sel[...], part) for part in split(dst[phase], 3))
        row8 = sum(lanes(got[KP * (t + 1) : KP * (t + 2)], -PIECE * t) for t in range(3))
        row8 = jnp.where(lane < PIECE, row8, 0.0)
        return jnp.concatenate([got[0:KP], row8], axis=0)

    def send_deliver(phase, own, dots):
        rows = [own[0:KP]] + [lanes(own[KP:], PIECE * t) for t in range(3)]
        rows.append(jnp.zeros((128 - 4 * KP, 128), F32))
        stacked = jnp.concatenate(rows, axis=0)
        out = sum(dot(selt[...], part) for part in split(stacked, 3))
        note = jnp.zeros((1, 128), F32)
        for i, value in enumerate(dots):
            note = jnp.where(lane == SCAL + i, value, note)
        out = out + jnp.where(iota((512, 128), 0) % 4 == 3, note, 0.0)
        src[phase] = out
        send(phase)

    def recv_deliver(phase, to_ref):
        arrived(phase)
        notes = jnp.zeros((8, 128), F32)
        for half in range(2):
            for r in range(8):
                for j in range(3):
                    to_ref[r * HI + j * 8 : r * HI + j * 8 + 8, half * 128 : half * 128 + 128] = dst[
                        phase, pl.ds(r * 64 + half * 32 + j, 8, stride=4), :
                    ]
            last = [jnp.zeros((8, 128), F32)] * 3
            for p in range(NP):
                row = dst[phase, pl.ds(p * 64 + half * 32 + 3, 8, stride=4), :]
                notes = notes + row
                for j in range(3):
                    last[j] = jnp.where(lane // PIECE == p, lanes(row, PIECE * (p - j)), last[j])
            for j in range(3):
                to_ref[8 * HI + j * 8 : 8 * HI + j * 8 + 8, half * 128 : half * 128 + 128] = last[j]
        notes = jnp.sum(notes, axis=0, keepdims=True)
        return [jnp.sum(jnp.where(lane == SCAL + i, notes, 0.0), axis=1, keepdims=True) for i in range(4)]

    def load_columns(x, parts):
        for i, part in enumerate(split(x, parts)):
            cols[i] = part

    def gather(b, k, parts):
        hid = hid_ref[b]
        for v in range(VIEWS):
            column = hot[b, :, v * PB : (v + 1) * PB]
            found = sum(dot(cols[i], column) for i in range(parts))
            mask = jnp.broadcast_to(hid[v : v + 1, :], (HI, PB)) == iota((HI, PB), 0)
            for r in range(ROWS):
                piece = found[r * HI : (r + 1) * HI]
                gath[k, r, v : v + 1, :] = jnp.sum(jnp.where(mask, piece, 0.0), axis=0, keepdims=True)

    def scatter(b, k, terms, to_ref):
        hid = hid_ref[b]
        count = len(terms)
        for r in range(count):
            top = terms[r].astype(BF16).astype(F32)
            terms_ref[k, r] = top
            terms_ref[k, count + r] = terms[r] - top
        for v in range(VIEWS):
            mask = jnp.broadcast_to(hid[v : v + 1, :], (HI, PB)) == iota((HI, PB), 0)
            for r in range(0, 2 * count, 2):
                rows = [jnp.broadcast_to(terms_ref[k, r + n, v : v + 1, :], (HI, PB)) for n in range(2)]
                both = jnp.concatenate([jnp.where(mask, row, 0.0) for row in rows], axis=0)
                t_ref[k, r * HI : (r + 2) * HI, v * PB : (v + 1) * PB] = both.astype(BF16)
        both = dot_nt(t_ref[k, 0 : 2 * count * HI], hot[b])
        to_ref[0 : count * HI] += both[0 : count * HI] + both[count * HI :]

    for half in range(2):
        for j in range(3):
            for r in range(8):
                d_ref[r * HI + j * 8 : r * HI + j * 8 + 8, half * 128 : half * 128 + 128] = dst0[
                    pl.ds(half * 256 + j * 8 + r, 8, stride=32), :
                ]
            d_ref[8 * HI + j * 8 : 8 * HI + j * 8 + 8, half * 128 : half * 128 + 128] = dst0[
                pl.ds(half * 256 + 24 + j, 8, stride=32), :
            ]
    load_columns(d_ref[...], 3)
    acc[...] = jnp.zeros_like(acc)

    def linearize(b, k):
        at = pl.ds(pl.multiple_of(b * PB, PB), PB)
        cams = [gath[k, r] for r in range(ROWS)]
        point = tuple(jnp.broadcast_to(pts_ref[i : i + 1, at], (VIEWS, PB)) for i in range(3))
        jac_cam, jac_pnt, value = jacobians(cams, point)
        residual = [value[i] - meas_ref[i, :, at] for i in range(2)]
        inv = inverse3(jac_pnt)
        grad = [
            -jnp.sum(jac_pnt[0][n] * residual[0] + jac_pnt[1][n] * residual[1], axis=0, keepdims=True)
            for n in range(3)
        ]
        moved = apply_inverse(inv, grad)
        for i in range(2):
            for r in range(ROWS):
                jc_ref[b, i * ROWS + r] = jac_cam[i][r]
            for n in range(3):
                jp_ref[b, i * 3 + n] = jac_pnt[i][n]
        for n in range(6):
            inv_ref[b, n : n + 1, :] = inv[n]
        for n in range(3):
            grad_ref[b, n : n + 1, :] = grad[n]
        left = [-residual[i] - dot3(jac_pnt[i], moved) for i in range(2)]
        squares = [jac_cam[0][r] * jac_cam[0][r] + jac_cam[1][r] * jac_cam[1][r] for r in range(ROWS)]
        scatter(b, k, squares + [jac_cam[0][r] * left[0] + jac_cam[1][r] * left[1] for r in range(ROWS)], acc)

    def linearize_group(group, _):
        for k in range(STEP):
            gather(STEP * group + k, k, 3)
        for k in range(STEP):
            linearize(STEP * group + k, k)
        return 0

    lax.fori_loop(0, NB // STEP, linearize_group, 0)
    send_collect(0, acc.at[0:SL])
    send_collect(1, acc.at[SL : 2 * SL])
    precond = recv_collect(0) + DAMPING
    remain = recv_collect(1)
    scaled = remain / precond
    direction = scaled
    send_deliver(2, scaled, [total(remain * scaled)])

    norm = recv_deliver(2, z_ref)[0]
    d_ref[...] = z_ref[...]

    def image_of(b, k, step):
        jac = [[jc_ref[b, i * ROWS + r] for r in range(ROWS)] for i in range(2)]
        jac_pnt = [[jp_ref[b, i * 3 + n] for n in range(3)] for i in range(2)]
        u = []
        for i in range(2):
            value = jac[i][0] * gath[k, 0]
            for r in range(1, ROWS):
                value = value + jac[i][r] * gath[k, r]
            u.append(value)
        w = [jnp.sum(jac_pnt[0][n] * u[0] + jac_pnt[1][n] * u[1], axis=0, keepdims=True) for n in range(3)]
        moved = apply_inverse([inv_ref[b, n : n + 1, :] for n in range(6)], w)
        left = [u[i] - dot3(jac_pnt[i], moved) for i in range(2)]
        return jac, u, w, moved, left

    def apply(group, step):
        for k in range(STEP):
            gather(STEP * group + k, k, 2)
        for k in range(STEP):
            b = STEP * group + k
            jac, _, w, _, left = image_of(b, k, step)
            for n in range(3):
                w_ref[step, b, n : n + 1, :] = w[n]
            scatter(b, k, [jac[0][r] * left[0] + jac[1][r] * left[1] for r in range(ROWS)], acc)
        return 0

    solved = None
    alphas = []
    for step in range(2):
        load_columns(d_ref[...], 2)
        acc[0:SL] = jnp.zeros((SL, 256), F32)
        lax.fori_loop(0, NB // STEP, lambda group, _: apply(group, step), 0)
        send_collect(3 + 2 * step, acc.at[0:SL])
        image = recv_collect(3 + 2 * step) + DAMPING * direction
        quot = image / precond
        send_deliver(
            4 + 2 * step, quot,
            [total(remain * scaled), total(direction * image), total(scaled * image), total(quot * image)],
        )
        rz, dim, zim, imq = recv_deliver(4 + 2 * step, acc2)
        alpha = rz / dim
        beta = (rz - 2.0 * alpha * zim + alpha * alpha * imq) / rz
        z_ref[...] = z_ref[...] - alpha * acc2[...]
        d_ref[...] = z_ref[...] + beta * d_ref[...]
        solved = alpha * direction if step == 0 else solved + alpha * direction
        remain = remain - alpha * image
        scaled = remain / precond
        direction = scaled + beta * direction
        alphas.append(alpha)

    srcx[0:KP] = solved[0:KP]
    srcx[KP : 2 * KP] = direction[0:KP]
    srcx[2 * KP :] = solved[KP:] + lanes(direction[KP:], PIECE)
    for offset in COLUMN:
        p, _ = there(offset)
        pltpu.make_async_remote_copy(
            srcx, message(dstx, pts, 3 * KP), semx.at[0], semx.at[1], device_id=(p, cam), device_id_type=MESH
        ).start()
    pltpu.make_async_copy(srcx, message(dstx, pts, 3 * KP), semx.at[1]).start()
    load_columns(d_ref[...], 2)
    uq[...] = jnp.zeros_like(uq)

    def finish(b, k):
        _, u, _, moved, left = image_of(b, k, 2)
        uq[...] += u[0] * left[0] + u[1] * left[1]
        rest = []
        for n in range(3):
            value = grad_ref[b, n : n + 1, :]
            for step in range(2):
                value = value - alphas[step] * w_ref[step, b, n : n + 1, :]
            rest.append(value)
        rest = apply_inverse([inv_ref[b, n : n + 1, :] for n in range(6)], rest)
        at = pl.ds(pl.multiple_of(b * PB, PB), PB)
        for n in range(3):
            p0_ref[n : n + 1, at] = rest[n]
            p2_ref[n : n + 1, at] = moved[n]

    def finish_group(group, _):
        for k in range(STEP):
            gather(STEP * group + k, k, 2)
        for k in range(STEP):
            finish(STEP * group + k, k)
        return 0

    lax.fori_loop(0, NB // STEP, finish_group, 0)
    mine = total(uq[...]) + DAMPING * total(direction * direction)
    norm = total(remain * scaled)
    fsrc[...] = jnp.where(lane == 0, mine, jnp.where(lane == 1, norm, 0.0)).reshape(1, 1, 128)
    for offset in OFFSETS:
        p, c = there(offset)
        pltpu.make_async_remote_copy(
            fsrc.at[0], fdst.at[me], fsem.at[0], fsem.at[1], device_id=(p, c), device_id_type=MESH
        ).start()
    fdst[me] = fsrc[0]

    pltpu.make_async_copy(dstx, dstx, semx.at[1]).wait()
    for part, out in ((0, s1o), (1, d2o)):
        tail = jnp.zeros((KP, 128), F32)
        for p in range(NP):
            tail = jnp.where(lane // PIECE == p, lanes(dstx[p * 3 * KP + 2 * KP : (p + 1) * 3 * KP], PIECE * (p - part)), tail)
        for k in range(TILES):
            out[0:8, k * 128 : (k + 1) * 128] = dstx[pl.ds(part * KP + k, 8, stride=3 * KP), :]
            out[8:9, k * 128 : (k + 1) * 128] = tail[k : k + 1]

    pltpu.make_async_copy(fdst.at[pl.ds(0, ND - 1)], fdst.at[pl.ds(0, ND - 1)], fsem.at[1]).wait()
    sums = jnp.sum(fdst[...], axis=0)
    dim = jnp.sum(jnp.where(lane == 0, sums, 0.0), axis=1, keepdims=True)
    rz = jnp.sum(jnp.where(lane == 1, sums, 0.0), axis=1, keepdims=True)
    alpha = rz / dim
    cam_out[...] = s1o[...] + alpha * d2o[...]
    pnt_out[...] = p0_ref[...] - alpha * p2_ref[...]

    pltpu.make_async_copy(src0.at[pl.ds(0, 480)], dst0.at[pl.ds(0, 480)], sem0.at[0]).wait()
    for phase in range(PHASES):
        sent(phase)
    rest = pl.ds(0, 7 * 3 * KP)
    pltpu.make_async_copy(dstx.at[rest], dstx.at[rest], semx.at[0]).wait()
    pltpu.make_async_copy(fdst.at[pl.ds(0, ND - 1)], fdst.at[pl.ds(0, ND - 1)], fsem.at[0]).wait()


def shards(cam_params, points, measured, obs_slot, vis_tiles):
    vmem = pl.BlockSpec(memory_space=pltpu.VMEM)
    dma = pltpu.SemaphoreType.DMA
    return pl.pallas_call(
        kernel,
        out_shape=(
            jax.ShapeDtypeStruct(cam_params.shape, F32),
            jax.ShapeDtypeStruct(points.shape, F32),
        ),
        in_specs=[pl.BlockSpec(memory_space=pl.ANY)] * 5,
        out_specs=(vmem, vmem),
        scratch_shapes=[
            pltpu.SMEM(vis_tiles.shape[::-1], jnp.int32),
            pltpu.VMEM(vis_tiles.shape[::-1], jnp.int32),
            pltpu.VMEM(cam_params.shape, F32),
            pltpu.VMEM(points.shape, F32),
            pltpu.VMEM(measured.shape, F32),
            pltpu.VMEM(obs_slot.shape, jnp.int32),
            pltpu.VMEM((TILES, 16, 128), F32),
            pltpu.VMEM((NC * 32, 128), F32),
            pltpu.VMEM((NC * 32, 128), F32),
            pltpu.VMEM((PHASES, ND * 4, 128), F32),
            pltpu.VMEM((PHASES, ND * 4, 128), F32),
            pltpu.VMEM((1, 1, 128), F32),
            pltpu.VMEM((ND, 1, 128), F32),
            pltpu.VMEM((3 * KP, 128), F32),
            pltpu.VMEM((NP * 3 * KP, 128), F32),
            pltpu.VMEM((NB, 256, OB), BF16),
            pltpu.VMEM((NB, VIEWS, PB), jnp.int32),
            pltpu.VMEM((STEP, 4 * SL, OB), BF16),
            pltpu.VMEM((NB, 2 * ROWS, VIEWS, PB), F32),
            pltpu.VMEM((NB, 6, VIEWS, PB), F32),
            pltpu.VMEM((NB, 8, PB), F32),
            pltpu.VMEM((NB, 8, PB), F32),
            pltpu.VMEM((2, NB, 8, PB), F32),
            pltpu.VMEM((STEP, 4 * ROWS, VIEWS, PB), F32),
            pltpu.VMEM((STEP, ROWS, VIEWS, PB), F32),
            pltpu.VMEM((3, SL, 256), BF16),
            pltpu.VMEM((2 * SL, 256), F32),
            pltpu.VMEM((SL, 256), F32),
            pltpu.VMEM((SL, 256), F32),
            pltpu.VMEM((SL, 256), F32),
            pltpu.VMEM((128, 512), BF16),
            pltpu.VMEM((512, 128), BF16),
            pltpu.VMEM((ROWS, TILES * 128), F32),
            pltpu.VMEM((ROWS, TILES * 128), F32),
            pltpu.VMEM((3, NB * PB), F32),
            pltpu.VMEM((3, NB * PB), F32),
            pltpu.VMEM((VIEWS, PB), F32),
            dma((6,)),
            dma((2,)),
            dma((PHASES,)),
            dma((PHASES,)),
            dma((2,)),
            dma((2,)),
            pltpu.SemaphoreType.REGULAR,
        ],
        compiler_params=pltpu.CompilerParams(
            collective_id=0, has_side_effects=True, vmem_limit_bytes=60 << 20
        ),
    )(vis_tiles.T, cam_params, points, measured, obs_slot)


def solution(mesh):
    placed = (
        P(None, "cam"),
        P(None, ("pts", "cam")),
        P(None, None, ("pts", "cam")),
        P(None, ("pts", "cam")),
        P(),
    )
    return jax.shard_map(
        shards,
        mesh=mesh,
        in_specs=placed,
        out_specs=(P(None, "cam"), P(None, ("pts", "cam"))),
        check_vma=False,
    )
```
